128 devices in a mesh: elem: 64 (over z, y_lo, x, core), section: 2 (over y_hi).
Axes of the slice: x: 4, y: 4 (y_hi: 2, y_lo: 2; y = y_hi * 2 + y_lo), z: 4, core: 2. Of those that a mesh axis runs over, the one named last changes fastest.
Arguments:
- u_start: float32 [2048, 320], P('elem'), may hold values from -6 to 6
- inverses: float32 [2048, 320, 320], P('elem'), may hold values from -1 to 2
- neighbours: int32 [2048, 5], P('elem'), may hold values from 0 to 2047, as said below
- partners: int32 [2048], replicated, may hold values from 0 to 2047, as said below
Outputs:
- section_states: float32 [4, 2048, 320], P('section', 'elem')
The draws below stay inside these ranges and needn't reach their ends.
Inputs may be any that keep to these rules, and one draw needn't show every extreme that they name: `neighbours`: every entry names an element on the same device as the row's element, or on the device just before or after it along elem, cyclically. The partners of the 32 elements of device d along elem lie on devices d + 16 and d + 17, cyclically, 16 on each.
All inputs are finite; a program needn't handle non-finite values.
Results may differ from the reference program's by a relative error of at most 0.0001.
Values sent between devices are 32-bit elements; how exact they have to be, the bound alone decides.
No kernel may reach another device: no remote copies, remote signals or barrier semaphores. Data moves between devices by JAX's collectives and lax.ppermute only.
A program may use at most 64 MiB of HBM per device.

```python
import math
import jax
import jax.numpy as jnp
from jax import lax

NODE1 = 4
UNK = 320
SECTIONS = 4
NEWTON = 2
E_DEV = 32
NE = 2048


def draw_inverses(key, part):
    key_diag, key_off = jax.random.split(jax.random.fold_in(key, 11))
    diagonal_vals = jax.random.uniform(key_diag, (NE, UNK), jnp.float32, 0.6, 1.0)
    off_diag = jax.random.normal(key_off, (NE, UNK, UNK), jnp.float32) * (0.3 / UNK ** 0.5)
    return off_diag + diagonal_vals[:, :, None] * jnp.eye(UNK, dtype=jnp.float32)[None]


def draw_neighbours(key, part):
    devices = NE // E_DEV
    key_shift, key_local = jax.random.split(jax.random.fold_in(key, 23))
    shift_rows = jax.random.randint(key_shift, (NE, 5), -1, 2)
    owner_dev = (jnp.arange(NE, dtype=jnp.int32) // E_DEV)[:, None]
    target_dev = (owner_dev + shift_rows + devices) % devices
    local_rows = jax.random.randint(key_local, (NE, 5), 0, E_DEV)
    return (target_dev * E_DEV + local_rows).astype(jnp.int32)


def draw_partners(key, part):
    devices = NE // E_DEV
    rotation = devices // 4
    key_order, key_local = jax.random.split(jax.random.fold_in(key, 37))

    def slot_order(dev_key):
        return jax.random.permutation(dev_key, E_DEV)
    orders = jax.vmap(slot_order)(jax.random.split(key_order, devices))
    upper = (orders >= E_DEV // 2).astype(jnp.int32)
    device_ids = jnp.arange(devices, dtype=jnp.int32)[:, None]
    target_dev = (device_ids + rotation + upper) % devices
    local_rows = jax.random.randint(key_local, (devices, E_DEV), 0, E_DEV)
    return (target_dev * E_DEV + local_rows).reshape(NE).astype(jnp.int32)


def steps_of(key, shape, pieces, least, top_value):
    def one(axis_at, parts):
        draws = jax.random.uniform(jax.random.fold_in(jax.random.fold_in(key, 6), axis_at), (parts,), jnp.float32, least / len(pieces), top_value / len(pieces))
        return jnp.repeat(jnp.exp(draws), shape[axis_at] // parts).reshape((-1,) + (1,) * (len(shape) - axis_at - 1))

    factor_of = one(*pieces[0])
    for cut in pieces[1:]:
        factor_of = factor_of * one(*cut)
    return factor_of


def noise(rng, dims, scale, reach, cuts=(), kind=jnp.bfloat16):
    gain = steps_of(rng, dims, cuts, -0.22, 0.18) if cuts else 1.0
    result = jax.random.normal(rng, dims, jnp.float32) * scale * gain
    return jnp.minimum(jnp.maximum(result, -reach), reach).astype(kind)


def setup_inputs(seed: int = 0) -> dict:
    keys = jax.random.split(jax.random.key(seed), 5)
    u_start = noise(keys[0], (NE, UNK), 1.0, 6.0, ((0, 64),), jnp.float32)
    inverses = draw_inverses(jax.random.fold_in(keys[4], 71), 0)
    neighbours = draw_neighbours(jax.random.fold_in(keys[4], 71), 0)
    partners = draw_partners(jax.random.fold_in(keys[4], 71), 0)
    return dict(u_start=u_start, inverses=inverses, neighbours=neighbours, partners=partners)


time_step = 0.03
dissipation = 2.0
enthalpy_factor = 3.5
radau_nodes = [0.08858795951270394, 0.4094668644407347, 0.787659461760847, 1.0]

def lobatto():
    node_count = NODE1
    if node_count == 4:
        inner_value = 1.0 / math.sqrt(5.0)
        lobatto_nodes = [-1.0, -inner_value, inner_value, 1.0]
    else:
        lobatto_nodes = [-1.0, 1.0]
    products = []
    for row in range(node_count):
        value = 1.0
        for other in range(node_count):
            if other != row:
                value = value * (lobatto_nodes[row] - lobatto_nodes[other])
        products.append(value)
    derivative = []
    for row in range(node_count):
        entries = []
        for column in range(node_count):
            if row == column:
                total = 0.0
                for other in range(node_count):
                    if other != row:
                        total = total + 1.0 / (lobatto_nodes[row] - lobatto_nodes[other])
                entries.append(2.0 * total)
            else:
                entries.append(2.0 * (products[row] / products[column]) / (lobatto_nodes[row] - lobatto_nodes[column]))
        derivative.append(entries)
    return (jnp.asarray(derivative, jnp.float32), float(node_count * (node_count - 1) / 2.0))

def radau_table():
    section_total = SECTIONS
    butcher = []
    columns = []
    for column in range(section_total):
        coeffs = [1.0]
        scale = 1.0
        for other in range(section_total):
            if other != column:
                shifted = [0.0] + coeffs
                for position in range(len(coeffs)):
                    shifted[position] = shifted[position] - radau_nodes[other] * coeffs[position]
                coeffs = shifted
                scale = scale * (radau_nodes[column] - radau_nodes[other])
        integral = [0.0] + [coeffs[position] / (position + 1.0) / scale for position in range(len(coeffs))]
        columns.append(integral)
    for row in range(section_total):
        entries = []
        for column in range(section_total):
            value = 0.0
            for coefficient in reversed(columns[column]):
                value = value * radau_nodes[row] + coefficient
            entries.append(value)
        butcher.append(entries)
    return butcher

def flux(left_state, right_state, direction):
    density = 0.5 * (left_state[:, :, 0] + right_state[:, :, 0])
    velocity = [0.5 * (left_state[:, :, 1 + comp] + right_state[:, :, 1 + comp]) for comp in range(3)]
    pressure = 0.5 * (left_state[:, :, 4] + right_state[:, :, 4])
    kinetic = 0.0
    for comp in range(3):
        kinetic = kinetic + 0.5 * (left_state[:, :, 1 + comp] ** 2 + right_state[:, :, 1 + comp] ** 2)
    normal_speed = velocity[direction]
    mass_flux = density * normal_speed
    components = [mass_flux]
    for comp in range(3):
        momentum = mass_flux * velocity[comp]
        if comp == direction:
            momentum = momentum + pressure
        components.append(momentum)
    components.append(enthalpy_factor * pressure * normal_speed + 0.5 * mass_flux * kinetic)
    return jnp.stack(components, axis=2)

def face_list(node_grid):
    return [node_grid[:, :, :, 0], node_grid[:, :, :, -1], node_grid[:, :, :, :, 0], node_grid[:, :, :, :, -1], node_grid[:, :, :, :, :, 0], node_grid[:, :, :, :, :, -1]]

def lift(faces):
    shape = faces[0].shape[:3] + (NODE1, NODE1, NODE1)
    node_grid = jnp.zeros(shape, jnp.float32)
    node_grid = node_grid.at[:, :, :, 0].add(faces[0]).at[:, :, :, -1].add(faces[1])
    node_grid = node_grid.at[:, :, :, :, 0].add(faces[2]).at[:, :, :, :, -1].add(faces[3])
    node_grid = node_grid.at[:, :, :, :, :, 0].add(faces[4]).at[:, :, :, :, :, -1].add(faces[5])
    return node_grid

def traces(states):
    node_grid = states.reshape(states.shape[0], states.shape[1], 5, NODE1, NODE1, NODE1)
    return jnp.stack([face.reshape(states.shape[0], states.shape[1], -1) for face in face_list(node_grid)], axis=2)

def split_faces(neighbour_faces):
    return [neighbour_faces[:, :, face_index].reshape(neighbour_faces.shape[0], neighbour_faces.shape[1], 5, NODE1, NODE1) for face_index in range(6)]

def tendency(states, neighbour_faces, double_deriv, inv_weight):
    highest = lax.Precision.HIGHEST
    node_grid = states.reshape(states.shape[0], states.shape[1], 5, NODE1, NODE1, NODE1)
    flux_x = flux(node_grid[:, :, :, :, None, :, :], node_grid[:, :, :, None, :, :, :], 0)
    combined = jnp.einsum('il,seailjk->seaijk', double_deriv, flux_x, precision=highest)
    flux_y = flux(node_grid[:, :, :, :, :, None, :], node_grid[:, :, :, :, None, :, :], 1)
    combined = combined + jnp.einsum('jm,seaijmk->seaijk', double_deriv, flux_y, precision=highest)
    flux_z = flux(node_grid[:, :, :, :, :, :, None], node_grid[:, :, :, :, :, None, :], 2)
    combined = combined + jnp.einsum('kn,seaijkn->seaijk', double_deriv, flux_z, precision=highest)
    own_faces = face_list(node_grid)
    other_faces = split_faces(neighbour_faces)
    corrections = []
    for face_index in range(6):
        direction = face_index // 2
        normal_sign = 2.0 * (face_index % 2) - 1.0
        own_face = own_faces[face_index]
        other_face = other_faces[face_index]
        jump = flux(own_face, other_face, direction) - flux(own_face, own_face, direction)
        corrections.append(normal_sign * jump - 0.5 * dissipation * (other_face - own_face))
    combined = combined + inv_weight * lift(corrections)
    return (-2.0 * combined).reshape(states.shape)

def apply_inverse(inverses, vectors):
    return jnp.einsum('epq,seq->sep', inverses, vectors, precision=lax.Precision.HIGHEST)

def reference(u_start, inverses, neighbours, partners):
    double_deriv, inv_weight = lobatto()
    butcher = jnp.asarray(radau_table(), jnp.float32)
    coupling = time_step * jnp.diagonal(butcher) * dissipation * inv_weight
    opposite = [1, 0, 3, 2, 5]

    def gather_faces(face_traces):
        picked = [face_traces[:, neighbours[:, face_index], opposite[face_index]] for face_index in range(5)]
        picked.append(face_traces[:, partners, 4])
        return jnp.stack(picked, axis=2)
    states = jnp.broadcast_to(u_start[None], (SECTIONS,) + u_start.shape).astype(jnp.float32)
    for newton_round in range(NEWTON):
        tendencies = tendency(states, gather_faces(traces(states)), double_deriv, inv_weight)
        coupled = jnp.einsum('ij,jep->iep', butcher, tendencies, precision=lax.Precision.HIGHEST)
        residual = states - u_start[None] - time_step * coupled
        first_sweep = apply_inverse(inverses, -residual)
        lifted = lift(split_faces(gather_faces(traces(first_sweep)))).reshape(states.shape)
        second = apply_inverse(inverses, -residual + coupling[:, None, None] * lifted)
        states = states + second
    return states
```

```python
import functools
import math

import jax
import jax.numpy as jnp
from jax import lax
from jax.experimental import pallas as pl
from jax.experimental.pallas import tpu as pltpu
from jax.sharding import PartitionSpec as P

ELEMS = 32
FIELDS = 5
UNK = 320
ROWS = 80
LANES = 128
GROUPS = 10
SECTIONS = 4

time_step = 0.03
dissipation = 2.0
enthalpy_factor = 3.5
radau_nodes = [0.08858795951270394, 0.4094668644407347, 0.787659461760847, 1.0]


def lobatto():
    inner = 1.0 / math.sqrt(5.0)
    nodes = [-1.0, -inner, inner, 1.0]
    products = []
    for row in range(4):
        value = 1.0
        for other in range(4):
            if other != row:
                value = value * (nodes[row] - nodes[other])
        products.append(value)
    return [
        [
            0.0 if row == column
            else 2.0 * (products[row] / products[column]) / (nodes[row] - nodes[column])
            for column in range(4)
        ]
        for row in range(4)
    ]


def radau_table():
    columns = []
    for column in range(SECTIONS):
        coeffs = [1.0]
        scale = 1.0
        for other in range(SECTIONS):
            if other != column:
                shifted = [0.0] + coeffs
                for position in range(len(coeffs)):
                    shifted[position] = shifted[position] - radau_nodes[other] * coeffs[position]
                coeffs = shifted
                scale = scale * (radau_nodes[column] - radau_nodes[other])
        columns.append([0.0] + [c / (k + 1.0) / scale for k, c in enumerate(coeffs)])
    butcher = []
    for row in range(SECTIONS):
        entries = []
        for column in range(SECTIONS):
            value = 0.0
            for coefficient in reversed(columns[column]):
                value = value * radau_nodes[row] + coefficient
            entries.append(value)
        butcher.append(entries)
    return butcher


DERIV = lobatto()
WEIGHT = 6.0
BUTCHER = radau_table()
ROW_SUM = [sum(row) for row in BUTCHER]
COUPLING = [time_step * BUTCHER[i][i] * dissipation * WEIGHT for i in range(SECTIONS)]
STEP_X = [time_step * ROW_SUM[i] for i in range(SECTIONS)]
STEP_Y = [time_step * ROW_SUM[i] * COUPLING[i] for i in range(SECTIONS)]


def sublane():
    return lax.broadcasted_iota(jnp.int32, (8, LANES), 0)


def lane():
    return lax.broadcasted_iota(jnp.int32, (8, LANES), 1)


def by_row(values):
    s = sublane()
    out = jnp.full((8, LANES), values[7], jnp.float32)
    for row in range(6, -1, -1):
        out = jnp.where(s == row, values[row], out)
    return out


def by_group(values):
    group = lane() // 32
    out = jnp.full((8, LANES), values[3], jnp.float32)
    for g in range(2, -1, -1):
        out = jnp.where(group == g, values[g], out)
    return out


def roll_rows(x, shift):
    shape = x.shape
    y = x.reshape(-1, 8, LANES)
    return pltpu.roll(y, shift % 8, axis=1).reshape(shape)


def roll_lanes(x, shift):
    if shift % LANES == 0:
        return x
    shape = x.shape
    y = x.reshape(-1, LANES)
    return pltpu.roll(y, shift % LANES, axis=1).reshape(shape)


def pick_lanes(x, index):
    shape = x.shape
    y = x.reshape(-1, LANES)
    wide = jnp.broadcast_to(index[None], (y.shape[0] // 8, 8, LANES)).reshape(y.shape)
    return jnp.take_along_axis(y, wide, axis=1, mode="promise_in_bounds").reshape(shape)


def prepared(u):
    half = [0.5 * u[f] for f in range(FIELDS)]
    square = half[1] * half[1] + half[2] * half[2] + half[3] * half[3]
    return half + [enthalpy_factor * half[4], square]


def take(state, index):
    return [x[index] for x in state]


def pair_flux(a, b, direction):
    density, v0, v1, v2, pressure, energy, square = [x + y for x, y in zip(a, b)]
    velocity = [v0, v1, v2]
    normal = velocity[direction]
    mass = density * normal
    out = [mass]
    for comp in range(3):
        momentum = mass * velocity[comp]
        out.append(momentum + pressure if comp == direction else momentum)
    out.append(normal * (energy + density * square))
    return out


def volume(u):
    n = prepared(u)
    d = DERIV
    rows = [[None] * 4 for _ in range(FIELDS)]

    def add(f, i, value):
        rows[f][i] = value if rows[f][i] is None else rows[f][i] + value

    for i in range(4):
        for other in range(i + 1, 4):
            flux = pair_flux(take(n, i), take(n, other), 0)
            for f in range(FIELDS):
                add(f, i, d[i][other] * flux[f])
                add(f, other, d[other][i] * flux[f])
    low = [(s // 4) for s in range(8)]
    c_same_low = by_row([d[j][1 - j] for j in low])
    c_same_high = by_row([d[2 + j][3 - j] for j in low])
    c_up = by_row([d[j][2 + j] for j in low])
    c_down = by_row([d[2 + j][j] for j in low])
    c_up_turn = by_row([d[j][3 - j] for j in low])
    c_down_turn = by_row([d[2 + j][1 - j] for j in low])
    c_next = [by_row([d[s % 4][(s % 4 + r) % 4] for s in range(8)]) for r in (1, 2, 3)]
    within = sublane() % 4

    def spin(x, r):
        return jnp.where(within + r < 4, roll_rows(x, 8 - r), roll_rows(x, 4 - r))

    for i in range(4):
        a = [x[i, 0] for x in n]
        b = [x[i, 1] for x in n]
        ra = [roll_rows(x, 4) for x in a]
        rb = [roll_rows(x, 4) for x in b]
        f1 = pair_flux(a, ra, 1)
        f2 = pair_flux(b, rb, 1)
        f3 = pair_flux(a, b, 1)
        f4 = pair_flux(a, rb, 1)
        f5 = pair_flux(b, ra, 1)
        n_i = [x[i] for x in n]
        z1 = pair_flux(n_i, [spin(x, 1) for x in n_i], 2)
        z2 = pair_flux(n_i, [spin(x, 2) for x in n_i], 2)
        for f in range(FIELDS):
            upper = c_same_low * f1[f] + c_up * f3[f] + c_up_turn * f4[f]
            lower = c_same_high * f2[f] + c_down * f3[f] + c_down_turn * f5[f]
            add(f, i, jnp.stack([upper, lower]))
            add(f, i, c_next[0] * z1[f] + c_next[1] * z2[f] + c_next[2] * spin(z1[f], 3))
    return jnp.stack([jnp.stack(rows[f]) for f in range(FIELDS)])


def face_terms(u, nx, ny, nz):
    n = prepared(u)
    px, py, pz = prepared(nx), prepared(ny), prepared(nz)
    half = 0.5 * dissipation
    s = sublane()
    low_x = pair_flux(take(n, 0), [x[0] for x in px], 0)
    high_x = pair_flux(take(n, 3), [x[1] for x in px], 0)
    y0 = pair_flux([x[:, 0] for x in n], [x[:, 0] for x in py], 1)
    y1 = pair_flux([x[:, 1] for x in n], [x[:, 1] for x in py], 1)
    z = pair_flux(n, pz, 2)
    k = s % 4
    sign_z = jnp.where(k == 0, -WEIGHT, WEIGHT)
    on_z = (k == 0) | (k == 3)
    out = []
    for f in range(FIELDS):
        part_z = jnp.where(on_z, sign_z * z[f] - (WEIGHT * half) * (nz[f] - u[f]), 0.0)
        part_y0 = jnp.where(s < 4, -WEIGHT * y0[f] - (WEIGHT * half) * (ny[f][:, 0] - u[f][:, 0]), 0.0)
        part_y1 = jnp.where(s < 4, 0.0, WEIGHT * y1[f] - (WEIGHT * half) * (ny[f][:, 1] - u[f][:, 1]))
        total = part_z + jnp.stack([part_y0, part_y1], axis=1)
        x0 = -WEIGHT * low_x[f] - (WEIGHT * half) * (nx[f][0] - u[f][0])
        x3 = WEIGHT * high_x[f] - (WEIGHT * half) * (nx[f][1] - u[f][3])
        out.append(jnp.stack([total[0] + x0, total[1], total[2], total[3] + x3]))
    return jnp.stack(out)


def lifted(nx, ny, nz):
    s = sublane()
    k = s % 4
    y = jnp.stack([jnp.where(s < 4, ny[:, :, 0], 0.0), jnp.where(s < 4, 0.0, ny[:, :, 1])], axis=2)
    total = y + jnp.where((k == 0) | (k == 3), nz, 0.0)
    return jnp.stack([total[:, 0] + nx[:, 0], total[:, 1], total[:, 2], total[:, 3] + nx[:, 1]], axis=1)


def aligned(near, far, index):
    nx = jnp.stack([pick_lanes(near[:, 3], index[0]), pick_lanes(near[:, 0], index[1])], axis=1)
    ny = jnp.stack(
        [
            roll_rows(pick_lanes(near[:, :, 1], index[2]), 4),
            roll_rows(pick_lanes(near[:, :, 0], index[3]), 4),
        ],
        axis=2,
    )
    lower = roll_rows(pick_lanes(near, index[4]), 5)
    upper = roll_rows(pick_lanes(far, index[5]), 3)
    nz = jnp.where(sublane() % 4 == 0, lower, upper)
    return nx, ny, nz


def nodes_of(parts):
    return jnp.stack([p.reshape(FIELDS, 2, 8, LANES) for p in parts], axis=1)


def group_of(x, groups):
    at = lane()[:1] // 32
    parts = [roll_lanes(y, 32 * (g - group)) for g, (y, group) in enumerate(zip(x, groups))]
    out = parts[-1]
    for g in range(len(parts) - 2, -1, -1):
        out = jnp.where(at == g, parts[g], out)
    return out


def near_far(before, own, after, ahead, beyond):
    near = nodes_of([group_of([before, own, after], [i] * 3) for i in range(4)])
    far = nodes_of([group_of([ahead, beyond], [i] * 2) for i in range(4)])
    return near, far


def spread(compact):
    base = lane() % 32
    return nodes_of([pick_lanes(compact, base + 32 * i) for i in range(4)])


def squeezed(nodes):
    at = lane() // 32
    parts = [nodes[:, i].reshape(ROWS // 8, 8, LANES) for i in range(4)]
    out = parts[3]
    for i in range(2, -1, -1):
        out = jnp.where(at == i, parts[i], out)
    return out.reshape(ROWS, LANES)


def flipped(x):
    pieces = [
        x[:, 0:128].T,
        x[:, 128:256].T,
        jnp.concatenate([x[:, 256:320], jnp.zeros((LANES, 64), jnp.float32)], axis=1).T[:64],
    ]
    return jnp.concatenate(pieces, axis=0).reshape(FIELDS, 4, 2, 8, LANES)


def multiply(t_ref, v_ref, out_ref, count, finish):
    def block(g, carry):
        rows = pl.ds(pl.multiple_of(g * 8, 8), 8)
        sums = [jnp.zeros((8, 8, LANES), jnp.float32) for _ in range(count)]
        for q in range(UNK // 8):
            piece = t_ref[rows, 8 * q : 8 * q + 8, :]
            for c in range(count):
                sums[c] = sums[c] + piece * v_ref[c, 8 * q : 8 * q + 8, :][None]
        for c in range(count):
            finish(c, rows, jnp.sum(sums[c], axis=1))
        return carry

    lax.fori_loop(0, GROUPS, block, 0)


def prepare_kernel(inv_ref, neighbours_ref, partners_ref, u_ref, t_ref, index_ref, nodes_ref, acc_ref, buf, square, sems):
    copies = []
    for g in range(GROUPS):
        f, half = g // 2, g % 2
        for i in range(4):
            start = f * 64 + i * 16 + half * 8
            copy = pltpu.make_async_copy(inv_ref.at[:, pl.ds(start, 8), :], buf.at[g, i], sems.at[g, i])
            copy.start()
            copies.append(copy)
    count = lax.axis_size("elem")
    rank = lax.axis_index("elem")
    square[...] = jnp.zeros((LANES, LANES), jnp.int32)
    square[0:ELEMS, 0:5] = neighbours_ref[...]
    turned = square[...].T[0:8, :]
    base = lane() % 32
    turned = jnp.take_along_axis(turned, base, axis=1, mode="promise_in_bounds")

    def slots(values, first):
        block = lax.shift_right_logical(values, 5) - rank - first
        block = jnp.where(block < 0, block + count, block)
        block = jnp.where(block < 0, block + count, block)
        block = jnp.where(block >= count, block - count, block)
        return block * ELEMS + (values & 31)

    near = slots(turned, -1)
    for face in range(5):
        index_ref[face] = jnp.broadcast_to(near[face : face + 1], (8, LANES))
    line = jnp.broadcast_to(partners_ref[pl.ds(rank // 4, 1), :], (8, LANES))
    line = jnp.take_along_axis(line, base + (rank % 4) * 32, axis=1, mode="promise_in_bounds")
    index_ref[5] = slots(line, count // 4)
    u = flipped(jnp.concatenate([u_ref[...]] * 4, axis=0))
    nodes_ref[...] = u
    acc_ref[...] = volume(u)

    def turn_group(g, carry):
        for i in range(4):
            pltpu.make_async_copy(inv_ref.at[:, pl.ds(0, 8), :], buf.at[g, i], sems.at[g, i]).wait()
        for r in range(8):
            x = buf[g, :, :, r, :].reshape(LANES, UNK)
            t_ref[g * 8 + r] = jnp.concatenate(
                [
                    x[:, 0:128].T,
                    x[:, 128:256].T,
                    jnp.concatenate([x[:, 256:320], x[:, 256:320]], axis=1).T[:64],
                ],
                axis=0,
            )
        return carry

    lax.fori_loop(0, GROUPS, turn_group, 0)


def first_kernel(t_ref, index_ref, nodes_ref, acc_ref, before_ref, own_ref, after_ref, ahead_ref, beyond_ref,
                 x_ref, nx_ref, ny_ref, nz_ref, v_ref):
    near = flipped(jnp.concatenate([before_ref[...], own_ref[...], after_ref[...], own_ref[...]], axis=0))
    far = flipped(jnp.concatenate([ahead_ref[...], beyond_ref[...]] * 2, axis=0))
    nx, ny, nz = aligned(near, far, index_ref[...])
    nx_ref[...], ny_ref[...], nz_ref[...] = nx, ny, nz
    total = acc_ref[...] + face_terms(nodes_ref[...], nx, ny, nz)
    v_ref[0] = (-2.0 * total).reshape(UNK, LANES)

    def finish(c, rows, value):
        x_ref[rows, :] = value

    multiply(t_ref, v_ref, x_ref, 1, finish)


def second_kernel(t_ref, index_ref, before_ref, own_ref, after_ref, ahead_ref, beyond_ref,
                  y_ref, nx_ref, ny_ref, nz_ref, v_ref):
    near, far = near_far(before_ref[...], own_ref[...], after_ref[...], ahead_ref[...], beyond_ref[...])
    nx, ny, nz = aligned(near, far, index_ref[...])
    nx_ref[...], ny_ref[...], nz_ref[...] = nx, ny, nz
    v_ref[0] = lifted(nx, ny, nz).reshape(UNK, LANES)

    def finish(c, rows, value):
        y_ref[rows, :] = value

    multiply(t_ref, v_ref, y_ref, 1, finish)


def middle_kernel(u_ref, x_ref, y_ref, states_ref, acc_ref):
    u = u_ref[...]
    x, y = spread(x_ref[...]), spread(y_ref[...])
    states = u + by_group(STEP_X) * x + by_group(STEP_Y) * y
    states_ref[...] = states
    acc_ref[...] = volume(states)


def section_value(table, which):
    first = lax.axis_index("section") == 0
    return jnp.where(first, table[which], table[2 + which]).astype(jnp.float32)


def third_kernel(t_ref, index_ref, u_ref, states_ref, acc_ref, x_ref,
                 ux_ref, uy_ref, uz_ref, xx_ref, xy_ref, xz_ref,
                 before_ref, own_ref, after_ref, ahead_ref, beyond_ref,
                 first_ref, base_ref, v_ref):
    near, far = near_far(before_ref[...], own_ref[...], after_ref[...], ahead_ref[...], beyond_ref[...])
    yx, yy, yz = aligned(near, far, index_ref[...])
    a, b = by_group(STEP_X), by_group(STEP_Y)
    nx = ux_ref[...] + a * xx_ref[...] + b * yx
    ny = uy_ref[...] + a * xy_ref[...] + b * yy
    nz = uz_ref[...] + a * xz_ref[...] + b * yz
    total = (acc_ref[...] + face_terms(states_ref[...], nx, ny, nz)).reshape(UNK, LANES)
    turned = [total] + [roll_lanes(total, 32 * r) for r in (1, 2, 3)]
    x, y = x_ref[...], own_ref[...]
    xs, ys = spread(x).reshape(UNK, LANES), spread(y).reshape(UNK, LANES)
    u = squeezed(u_ref[...])
    shape = (UNK // 8, 8, LANES)
    for c in range(2):
        v = -section_value(STEP_X, c) * xs - section_value(STEP_Y, c) * ys
        v = v.reshape(shape)
        for r in range(4):
            factor = by_group(
                [
                    section_value([-2.0 * time_step * BUTCHER[s][(g - r) % 4] for s in range(4)], c)
                    for g in range(4)
                ]
            )
            v = v + factor * turned[r].reshape(shape)
        v_ref[c] = v.reshape(UNK, LANES)
        base_ref[c] = u + section_value(STEP_X, c) * x + section_value(STEP_Y, c) * y

    def finish(c, rows, value):
        first_ref[c, rows, :] = value
        base_ref[c, rows, :] = base_ref[c, rows, :] + value

    multiply(t_ref, v_ref, first_ref, 2, finish)


def fourth_kernel(t_ref, index_ref, base_ref, before_ref, own_ref, after_ref, ahead_ref, beyond_ref, out_ref, v_ref, done_ref):
    for c in range(2):
        near, far = near_far(before_ref[c], own_ref[c], after_ref[c], ahead_ref[c], beyond_ref[c])
        v_ref[c] = lifted(*aligned(near, far, index_ref[...])).reshape(UNK, LANES)

    def finish(c, rows, value):
        done_ref[c, rows, :] = base_ref[c, rows, :] + section_value(COUPLING, c) * value

    multiply(t_ref, v_ref, done_ref, 2, finish)
    both = nodes_of([group_of([done_ref[0], done_ref[1]], [i] * 2) for i in range(4)]).reshape(UNK, LANES)
    turned = [
        both[0:128].T,
        both[128:256].T,
        jnp.concatenate([both[256:320], both[256:320]], axis=0).T[:, :64],
    ]
    for c in range(2):
        rows = slice(c * ELEMS, (c + 1) * ELEMS)
        out_ref[c, :, 0:128] = turned[0][rows]
        out_ref[c, :, 128:256] = turned[1][rows]
        out_ref[c, :, 256:320] = turned[2][rows]


VMEM = pltpu.VMEM
F32 = jnp.float32
NODES = (FIELDS, 4, 2, 8, LANES)
NX = (FIELDS, 2, 2, 8, LANES)
COMPACT = (ROWS, LANES)


def call(kernel, inputs, outputs, scratch=(), anywhere=(), flops=10**7, room=8):
    in_specs = [pl.BlockSpec(memory_space=pltpu.HBM if i in anywhere else VMEM) for i in range(len(inputs))]
    return pl.pallas_call(
        kernel,
        out_shape=outputs,
        in_specs=in_specs,
        out_specs=[pl.BlockSpec(memory_space=VMEM)] * len(outputs),
        scratch_shapes=list(scratch),
        compiler_params=pltpu.CompilerParams(vmem_limit_bytes=room * 2**20),
        cost_estimate=pl.CostEstimate(flops=flops, bytes_accessed=10**6, transcendentals=0),
    )(*inputs)


def vm(shape, dtype=F32):
    return pltpu.VMEM(shape, dtype)


def passed(block, distance):
    count = lax.axis_size("elem")
    return lax.ppermute(block, "elem", [((i - distance) % count, i) for i in range(count)])


def exchanged(block):
    far = lax.axis_size("elem") // 4
    before, after = passed(block, 1), passed(block, -1)
    ahead, beyond = passed(block, -far), passed(block, -(far + 1))
    return [before, block, after, ahead, beyond]


def keep(x):
    return pltpu.with_memory_space_constraint(x, VMEM)


def on_device(u_start, inverses, neighbours, partners):
    partners = partners.reshape(-1, LANES)
    u_all = exchanged(u_start)
    t, index, nodes, acc = call(
        prepare_kernel,
        [pltpu.with_memory_space_constraint(inverses, pltpu.HBM), neighbours, partners, u_start],
        [vm((ROWS, UNK, LANES)), vm((6, 8, LANES), jnp.int32), vm(NODES), vm(NODES)],
        [
            pltpu.VMEM((GROUPS, 4, ELEMS, 8, UNK), F32),
            pltpu.VMEM((LANES, LANES), jnp.int32),
            pltpu.SemaphoreType.DMA((GROUPS, 4)),
        ],
        anywhere=(0,),
        flops=10**9,
        room=24,
    )
    t, index, nodes = keep(t), keep(index), keep(nodes)
    x, ux, uy, uz = call(
        first_kernel, [t, index, nodes, keep(acc), *u_all],
        [vm(COMPACT), vm(NX), vm(NODES), vm(NODES)], [pltpu.VMEM((1, UNK, LANES), F32)],
    )
    y, xx, xy, xz = call(
        second_kernel, [t, index, *exchanged(x)],
        [vm(COMPACT), vm(NX), vm(NODES), vm(NODES)], [pltpu.VMEM((1, UNK, LANES), F32)],
    )
    y_all = exchanged(y)
    states, acc = call(middle_kernel, [nodes, x, y], [vm(NODES), vm(NODES)])
    first, base = call(
        third_kernel,
        [t, index, nodes, keep(states), keep(acc), x, *[keep(k) for k in (ux, uy, uz, xx, xy, xz)], *y_all],
        [vm((2,) + COMPACT), vm((2,) + COMPACT)], [pltpu.VMEM((2, UNK, LANES), F32)],
    )
    [out] = call(
        fourth_kernel, [t, index, keep(base), *exchanged(first)],
        [jax.ShapeDtypeStruct((2, ELEMS, UNK), F32)],
        [pltpu.VMEM((2, UNK, LANES), F32), pltpu.VMEM((2,) + COMPACT, F32)],
    )
    return out


def solution(mesh):
    placed = (P("elem", None), P("elem", None, None), P("elem", None), P())
    return jax.shard_map(
        on_device, mesh=mesh, in_specs=placed, out_specs=P("section", "elem", None), check_vma=False
    )
```

```python
import functools
import math

import jax
import jax.numpy as jnp
from jax import lax
from jax.experimental import pallas as pl
from jax.experimental.pallas import tpu as pltpu
from jax.sharding import PartitionSpec as P

ELEMS = 32
FIELDS = 5
UNK = 320
ROWS = 80
LANES = 128
GROUPS = 10
SECTIONS = 4

time_step = 0.03
dissipation = 2.0
enthalpy_factor = 3.5
radau_nodes = [0.08858795951270394, 0.4094668644407347, 0.787659461760847, 1.0]


def lobatto():
    inner = 1.0 / math.sqrt(5.0)
    nodes = [-1.0, -inner, inner, 1.0]
    products = []
    for row in range(4):
        value = 1.0
        for other in range(4):
            if other != row:
                value = value * (nodes[row] - nodes[other])
        products.append(value)
    return [
        [
            0.0 if row == column
            else 2.0 * (products[row] / products[column]) / (nodes[row] - nodes[column])
            for column in range(4)
        ]
        for row in range(4)
    ]


def radau_table():
    columns = []
    for column in range(SECTIONS):
        coeffs = [1.0]
        scale = 1.0
        for other in range(SECTIONS):
            if other != column:
                shifted = [0.0] + coeffs
                for position in range(len(coeffs)):
                    shifted[position] = shifted[position] - radau_nodes[other] * coeffs[position]
                coeffs = shifted
                scale = scale * (radau_nodes[column] - radau_nodes[other])
        columns.append([0.0] + [c / (k + 1.0) / scale for k, c in enumerate(coeffs)])
    butcher = []
    for row in range(SECTIONS):
        entries = []
        for column in range(SECTIONS):
            value = 0.0
            for coefficient in reversed(columns[column]):
                value = value * radau_nodes[row] + coefficient
            entries.append(value)
        butcher.append(entries)
    return butcher


DERIV = lobatto()
WEIGHT = 6.0
BUTCHER = radau_table()
ROW_SUM = [sum(row) for row in BUTCHER]
COUPLING = [time_step * BUTCHER[i][i] * dissipation * WEIGHT for i in range(SECTIONS)]
STEP_X = [time_step * ROW_SUM[i] for i in range(SECTIONS)]
STEP_Y = [time_step * ROW_SUM[i] * COUPLING[i] for i in range(SECTIONS)]


def sublane():
    return lax.broadcasted_iota(jnp.int32, (8, LANES), 0)


def lane():
    return lax.broadcasted_iota(jnp.int32, (8, LANES), 1)


def by_row(values):
    s = sublane()
    out = jnp.full((8, LANES), values[7], jnp.float32)
    for row in range(6, -1, -1):
        out = jnp.where(s == row, values[row], out)
    return out


def by_group(values):
    group = lane() // 32
    out = jnp.full((8, LANES), values[3], jnp.float32)
    for g in range(2, -1, -1):
        out = jnp.where(group == g, values[g], out)
    return out


def roll_rows(x, shift):
    shape = x.shape
    y = x.reshape(-1, 8, LANES)
    return pltpu.roll(y, shift % 8, axis=1).reshape(shape)


def roll_lanes(x, shift):
    if shift % LANES == 0:
        return x
    shape = x.shape
    y = x.reshape(-1, LANES)
    return pltpu.roll(y, shift % LANES, axis=1).reshape(shape)


def pick_lanes(x, index):
    shape = x.shape
    y = x.reshape(-1, LANES)
    wide = jnp.broadcast_to(index[None], (y.shape[0] // 8, 8, LANES)).reshape(y.shape)
    return jnp.take_along_axis(y, wide, axis=1, mode="promise_in_bounds").reshape(shape)


def prepared(u):
    half = [0.5 * u[f] for f in range(FIELDS)]
    square = half[1] * half[1] + half[2] * half[2] + half[3] * half[3]
    return half + [enthalpy_factor * half[4], square]


def take(state, index):
    return [x[index] for x in state]


def pair_flux(a, b, direction):
    density, v0, v1, v2, pressure, energy, square = [x + y for x, y in zip(a, b)]
    velocity = [v0, v1, v2]
    normal = velocity[direction]
    mass = density * normal
    out = [mass]
    for comp in range(3):
        momentum = mass * velocity[comp]
        out.append(momentum + pressure if comp == direction else momentum)
    out.append(normal * (energy + density * square))
    return out


def volume(u):
    n = prepared(u)
    d = DERIV
    rows = [[None] * 4 for _ in range(FIELDS)]

    def add(f, i, value):
        rows[f][i] = value if rows[f][i] is None else rows[f][i] + value

    for i in range(4):
        for other in range(i + 1, 4):
            flux = pair_flux(take(n, i), take(n, other), 0)
            for f in range(FIELDS):
                add(f, i, d[i][other] * flux[f])
                add(f, other, d[other][i] * flux[f])
    low = [(s // 4) for s in range(8)]
    c_same_low = by_row([d[j][1 - j] for j in low])
    c_same_high = by_row([d[2 + j][3 - j] for j in low])
    c_up = by_row([d[j][2 + j] for j in low])
    c_down = by_row([d[2 + j][j] for j in low])
    c_up_turn = by_row([d[j][3 - j] for j in low])
    c_down_turn = by_row([d[2 + j][1 - j] for j in low])
    c_next = [by_row([d[s % 4][(s % 4 + r) % 4] for s in range(8)]) for r in (1, 2, 3)]
    within = sublane() % 4

    def spin(x, r):
        return jnp.where(within + r < 4, roll_rows(x, 8 - r), roll_rows(x, 4 - r))

    for i in range(4):
        a = [x[i, 0] for x in n]
        b = [x[i, 1] for x in n]
        ra = [roll_rows(x, 4) for x in a]
        rb = [roll_rows(x, 4) for x in b]
        f1 = pair_flux(a, ra, 1)
        f2 = pair_flux(b, rb, 1)
        f3 = pair_flux(a, b, 1)
        f4 = pair_flux(a, rb, 1)
        f5 = pair_flux(b, ra, 1)
        n_i = [x[i] for x in n]
        z1 = pair_flux(n_i, [spin(x, 1) for x in n_i], 2)
        z2 = pair_flux(n_i, [spin(x, 2) for x in n_i], 2)
        for f in range(FIELDS):
            upper = c_same_low * f1[f] + c_up * f3[f] + c_up_turn * f4[f]
            lower = c_same_high * f2[f] + c_down * f3[f] + c_down_turn * f5[f]
            add(f, i, jnp.stack([upper, lower]))
            add(f, i, c_next[0] * z1[f] + c_next[1] * z2[f] + c_next[2] * spin(z1[f], 3))
    return jnp.stack([jnp.stack(rows[f]) for f in range(FIELDS)])


def face_terms(u, nx, ny, nz):
    n = prepared(u)
    px, py, pz = prepared(nx), prepared(ny), prepared(nz)
    half = 0.5 * dissipation
    s = sublane()
    low_x = pair_flux(take(n, 0), [x[0] for x in px], 0)
    high_x = pair_flux(take(n, 3), [x[1] for x in px], 0)
    y0 = pair_flux([x[:, 0] for x in n], [x[:, 0] for x in py], 1)
    y1 = pair_flux([x[:, 1] for x in n], [x[:, 1] for x in py], 1)
    z = pair_flux(n, pz, 2)
    k = s % 4
    sign_z = jnp.where(k == 0, -WEIGHT, WEIGHT)
    on_z = (k == 0) | (k == 3)
    out = []
    for f in range(FIELDS):
        part_z = jnp.where(on_z, sign_z * z[f] - (WEIGHT * half) * (nz[f] - u[f]), 0.0)
        part_y0 = jnp.where(s < 4, -WEIGHT * y0[f] - (WEIGHT * half) * (ny[f][:, 0] - u[f][:, 0]), 0.0)
        part_y1 = jnp.where(s < 4, 0.0, WEIGHT * y1[f] - (WEIGHT * half) * (ny[f][:, 1] - u[f][:, 1]))
        total = part_z + jnp.stack([part_y0, part_y1], axis=1)
        x0 = -WEIGHT * low_x[f] - (WEIGHT * half) * (nx[f][0] - u[f][0])
        x3 = WEIGHT * high_x[f] - (WEIGHT * half) * (nx[f][1] - u[f][3])
        out.append(jnp.stack([total[0] + x0, total[1], total[2], total[3] + x3]))
    return jnp.stack(out)


def lifted(nx, ny, nz):
    s = sublane()
    k = s % 4
    y = jnp.stack([jnp.where(s < 4, ny[:, :, 0], 0.0), jnp.where(s < 4, 0.0, ny[:, :, 1])], axis=2)
    total = y + jnp.where((k == 0) | (k == 3), nz, 0.0)
    return jnp.stack([total[:, 0] + nx[:, 0], total[:, 1], total[:, 2], total[:, 3] + nx[:, 1]], axis=1)


def aligned(near, far, index):
    nx = jnp.stack([pick_lanes(near[:, 3], index[0]), pick_lanes(near[:, 0], index[1])], axis=1)
    ny = jnp.stack(
        [
            roll_rows(pick_lanes(near[:, :, 1], index[2]), 4),
            roll_rows(pick_lanes(near[:, :, 0], index[3]), 4),
        ],
        axis=2,
    )
    lower = roll_rows(pick_lanes(near, index[4]), 5)
    upper = roll_rows(pick_lanes(far, index[5]), 3)
    nz = jnp.where(sublane() % 4 == 0, lower, upper)
    return nx, ny, nz


def nodes_of(parts):
    return jnp.stack([p.reshape(FIELDS, 2, 8, LANES) for p in parts], axis=1)


def group_of(x, groups):
    at = lane()[:1] // 32
    parts = [roll_lanes(y, 32 * (g - group)) for g, (y, group) in enumerate(zip(x, groups))]
    out = parts[-1]
    for g in range(len(parts) - 2, -1, -1):
        out = jnp.where(at == g, parts[g], out)
    return out


def near_far(before, own, after, ahead, beyond):
    near = nodes_of([group_of([before, own, after], [i] * 3) for i in range(4)])
    far = nodes_of([group_of([ahead, beyond], [i] * 2) for i in range(4)])
    return near, far


def spread(compact):
    base = lane() % 32
    return nodes_of([pick_lanes(compact, base + 32 * i) for i in range(4)])


def squeezed(nodes):
    at = lane() // 32
    parts = [nodes[:, i].reshape(ROWS // 8, 8, LANES) for i in range(4)]
    out = parts[3]
    for i in range(2, -1, -1):
        out = jnp.where(at == i, parts[i], out)
    return out.reshape(ROWS, LANES)


def flipped(x):
    pieces = [
        x[:, 0:128].T,
        x[:, 128:256].T,
        jnp.concatenate([x[:, 256:320], jnp.zeros((LANES, 64), jnp.float32)], axis=1).T[:64],
    ]
    return jnp.concatenate(pieces, axis=0).reshape(FIELDS, 4, 2, 8, LANES)


def multiply(t_ref, v_ref, out_ref, count, finish):
    def block(g, carry):
        rows = pl.ds(pl.multiple_of(g * 8, 8), 8)
        sums = [jnp.zeros((8, 8, LANES), jnp.float32) for _ in range(count)]
        for q in range(UNK // 8):
            piece = t_ref[rows, 8 * q : 8 * q + 8, :]
            for c in range(count):
                sums[c] = sums[c] + piece * v_ref[c, 8 * q : 8 * q + 8, :][None]
        for c in range(count):
            finish(c, rows, jnp.sum(sums[c], axis=1))
        return carry

    lax.fori_loop(0, GROUPS, block, 0)


def prepare_kernel(inv_ref, neighbours_ref, partners_ref, u_ref, t_ref, index_ref, nodes_ref, acc_ref,
                   wide, tail, square, line_ref, own, sems, small):
    smalls = [
        pltpu.make_async_copy(u_ref, own, small.at[0]),
        pltpu.make_async_copy(neighbours_ref, square, small.at[1]),
        pltpu.make_async_copy(partners_ref, line_ref, small.at[2]),
    ]
    for copy in smalls:
        copy.start()

    def pieces(g, i, start):
        rows = pl.ds(start, 8)
        return [
            pltpu.make_async_copy(inv_ref.at[:, rows, pl.ds(0, 128)], wide.at[g, 0, i], sems.at[g, i, 0]),
            pltpu.make_async_copy(inv_ref.at[:, rows, pl.ds(128, 128)], wide.at[g, 1, i], sems.at[g, i, 1]),
            pltpu.make_async_copy(inv_ref.at[:, rows, pl.ds(256, 64)], tail.at[g, i], sems.at[g, i, 2]),
        ]

    for g in range(GROUPS):
        f, half = g // 2, g % 2
        for i in range(4):
            for copy in pieces(g, i, f * 64 + i * 16 + half * 8):
                copy.start()
    for copy in smalls:
        copy.wait()
    count = lax.axis_size("elem")
    rank = lax.axis_index("elem")
    base = lane() % 32
    blank = jnp.zeros((ELEMS, LANES - 5), jnp.int32)
    padded = jnp.concatenate([square[...], blank], axis=1)
    turned = jnp.concatenate([padded] * 4, axis=0).T[0:8, :]

    def slots(values, first):
        block = lax.shift_right_logical(values, 5) - rank - first
        block = jnp.where(block < 0, block + count, block)
        block = jnp.where(block < 0, block + count, block)
        block = jnp.where(block >= count, block - count, block)
        return block * ELEMS + (values & 31)

    near = slots(turned, -1)
    for face in range(5):
        index_ref[face] = jnp.broadcast_to(near[face : face + 1], (8, LANES))
    line = jnp.broadcast_to(line_ref[pl.ds(rank // 4, 1), :], (8, LANES))
    line = jnp.take_along_axis(line, base + (rank % 4) * 32, axis=1, mode="promise_in_bounds")
    index_ref[5] = slots(line, count // 4)
    u = flipped(jnp.concatenate([own[...]] * 4, axis=0))
    nodes_ref[...] = u
    acc_ref[...] = volume(u)

    def turn_group(g, carry):
        for i in range(4):
            for copy in pieces(g, i, 0):
                copy.wait()
        for r in range(8):
            rows = pl.ds(r, LANES, stride=8)
            t_ref[g * 8 + r, 0:128] = wide.at[g, 0].reshape(1024, LANES)[rows, :].T
            t_ref[g * 8 + r, 128:256] = wide.at[g, 1].reshape(1024, LANES)[rows, :].T
            t_ref[g * 8 + r, 256:320] = tail[g, :, :, r, :].reshape(LANES, 64).T
        return carry

    lax.fori_loop(0, GROUPS, turn_group, 0)


def first_kernel(t_ref, index_ref, nodes_ref, acc_ref, beyond_ref, ahead_ref, after_ref, before_ref,
                 x_ref, nx_ref, ny_ref, nz_ref, v_ref):
    near = flipped(jnp.concatenate([before_ref[...], before_ref[...], after_ref[...], after_ref[...]], axis=0))
    near = jnp.where(lane() // 32 == 1, nodes_ref[...], near)
    far = flipped(jnp.concatenate([ahead_ref[...], beyond_ref[...]] * 2, axis=0))
    nx, ny, nz = aligned(near, far, index_ref[...])
    nx_ref[...], ny_ref[...], nz_ref[...] = nx, ny, nz
    total = acc_ref[...] + face_terms(nodes_ref[...], nx, ny, nz)
    v_ref[0] = (-2.0 * total).reshape(UNK, LANES)

    def finish(c, rows, value):
        x_ref[rows, :] = value

    multiply(t_ref, v_ref, x_ref, 1, finish)


def second_kernel(t_ref, index_ref, beyond_ref, ahead_ref, own_ref, after_ref, before_ref,
                  y_ref, nx_ref, ny_ref, nz_ref, v_ref):
    near, far = near_far(before_ref[...], own_ref[...], after_ref[...], ahead_ref[...], beyond_ref[...])
    nx, ny, nz = aligned(near, far, index_ref[...])
    nx_ref[...], ny_ref[...], nz_ref[...] = nx, ny, nz
    v_ref[0] = lifted(nx, ny, nz).reshape(UNK, LANES)

    def finish(c, rows, value):
        y_ref[rows, :] = value

    multiply(t_ref, v_ref, y_ref, 1, finish)


def section_value(table, which):
    first = lax.axis_index("section") == 0
    return jnp.where(first, table[which], table[2 + which]).astype(jnp.float32)


def middle_kernel(u_ref, x_ref, y_ref, ux_ref, uy_ref, uz_ref, xx_ref, xy_ref, xz_ref,
                  states_ref, acc_ref, nx_ref, ny_ref, nz_ref, part_ref, base_ref):
    u = u_ref[...]
    x, y = spread(x_ref[...]), spread(y_ref[...])
    a = by_group(STEP_X)
    states = u + a * x + by_group(STEP_Y) * y
    states_ref[...] = states
    acc_ref[...] = volume(states)
    nx_ref[...] = ux_ref[...] + a * xx_ref[...]
    ny_ref[...] = uy_ref[...] + a * xy_ref[...]
    nz_ref[...] = uz_ref[...] + a * xz_ref[...]
    compact = squeezed(u)
    for c in range(2):
        part_ref[c] = -section_value(STEP_X, c) * x - section_value(STEP_Y, c) * y
        base_ref[c] = compact + section_value(STEP_X, c) * x_ref[...] + section_value(STEP_Y, c) * y_ref[...]


def third_kernel(t_ref, index_ref, states_ref, acc_ref, nx_ref, ny_ref, nz_ref, part_ref, base_ref,
                 beyond_ref, ahead_ref, own_ref, after_ref, before_ref, first_ref, sum_ref, v_ref):
    near, far = near_far(before_ref[...], own_ref[...], after_ref[...], ahead_ref[...], beyond_ref[...])
    yx, yy, yz = aligned(near, far, index_ref[...])
    b = by_group(STEP_Y)
    total = acc_ref[...] + face_terms(
        states_ref[...], nx_ref[...] + b * yx, ny_ref[...] + b * yy, nz_ref[...] + b * yz
    )
    turned = [total] + [roll_lanes(total, 32 * r) for r in (1, 2, 3)]
    for c in range(2):
        v = part_ref[c]
        for r in range(4):
            factor = by_group(
                [
                    section_value([-2.0 * time_step * BUTCHER[s][(g - r) % 4] for s in range(4)], c)
                    for g in range(4)
                ]
            )
            v = v + factor * turned[r]
        v_ref[c] = v.reshape(UNK, LANES)

    def finish(c, rows, value):
        first_ref[c, rows, :] = value
        sum_ref[c, rows, :] = base_ref[c, rows, :] + value

    multiply(t_ref, v_ref, first_ref, 2, finish)


def fourth_kernel(t_ref, index_ref, base_ref, beyond_ref, ahead_ref, own_ref, after_ref, before_ref, out_ref, v_ref, done_ref):
    for c in range(2):
        near, far = near_far(before_ref[c], own_ref[c], after_ref[c], ahead_ref[c], beyond_ref[c])
        v_ref[c] = lifted(*aligned(near, far, index_ref[...])).reshape(UNK, LANES)

    def finish(c, rows, value):
        done_ref[c, rows, :] = base_ref[c, rows, :] + section_value(COUPLING, c) * value

    multiply(t_ref, v_ref, done_ref, 2, finish)
    both = nodes_of([group_of([done_ref[0], done_ref[1]], [i] * 2) for i in range(4)]).reshape(UNK, LANES)
    turned = [
        both[0:128].T,
        both[128:256].T,
        jnp.concatenate([both[256:320], both[256:320]], axis=0).T[:, :64],
    ]
    for c in range(2):
        rows = slice(c * ELEMS, (c + 1) * ELEMS)
        out_ref[c, :, 0:128] = turned[0][rows]
        out_ref[c, :, 128:256] = turned[1][rows]
        out_ref[c, :, 256:320] = turned[2][rows]


VMEM = pltpu.VMEM
F32 = jnp.float32
NODES = (FIELDS, 4, 2, 8, LANES)
NX = (FIELDS, 2, 2, 8, LANES)
COMPACT = (ROWS, LANES)


def call(kernel, inputs, outputs, scratch=(), anywhere=(), flops=10**7, room=8):
    in_specs = [pl.BlockSpec(memory_space=pltpu.HBM if i in anywhere else VMEM) for i in range(len(inputs))]
    return pl.pallas_call(
        kernel,
        out_shape=outputs,
        in_specs=in_specs,
        out_specs=[pl.BlockSpec(memory_space=VMEM)] * len(outputs),
        scratch_shapes=list(scratch),
        compiler_params=pltpu.CompilerParams(vmem_limit_bytes=room * 2**20),
        cost_estimate=pl.CostEstimate(flops=flops, bytes_accessed=10**6, transcendentals=0),
    )(*inputs)


def vm(shape, dtype=F32):
    return pltpu.VMEM(shape, dtype)


def passed(block, distance):
    count = lax.axis_size("elem")
    return lax.ppermute(block, "elem", [((i - distance) % count, i) for i in range(count)])


def exchanged(block):
    far = lax.axis_size("elem") // 4
    beyond, ahead = passed(block, -(far + 1)), passed(block, -far)
    after, before = passed(block, -1), passed(block, 1)
    return [beyond, ahead, block, after, before]


def keep(x):
    return pltpu.with_memory_space_constraint(x, VMEM)


def on_device(u_start, inverses, neighbours, partners):
    partners = partners.reshape(-1, LANES)
    u_all = exchanged(u_start)
    t, index, nodes, acc = call(
        prepare_kernel,
        [pltpu.with_memory_space_constraint(k, pltpu.HBM) for k in (inverses, neighbours, partners, u_start)],
        [vm((ROWS, UNK, LANES)), vm((6, 8, LANES), jnp.int32), vm(NODES), vm(NODES)],
        [
            pltpu.VMEM((GROUPS, 2, 4, ELEMS, 8, LANES), F32),
            pltpu.VMEM((GROUPS, 4, ELEMS, 8, 64), F32),
            pltpu.VMEM((ELEMS, 5), jnp.int32),
            pltpu.VMEM((partners.shape[0], LANES), jnp.int32),
            pltpu.VMEM((ELEMS, UNK), F32),
            pltpu.SemaphoreType.DMA((GROUPS, 4, 3)),
            pltpu.SemaphoreType.DMA((3,)),
        ],
        anywhere=(0, 1, 2, 3),
        flops=10**9,
        room=24,
    )
    t, index, nodes = keep(t), keep(index), keep(nodes)
    x, ux, uy, uz = call(
        first_kernel, [t, index, nodes, keep(acc), *u_all[:2], *u_all[3:]],
        [vm(COMPACT), vm(NX), vm(NODES), vm(NODES)], [pltpu.VMEM((1, UNK, LANES), F32)],
    )
    y, xx, xy, xz = call(
        second_kernel, [t, index, *exchanged(x)],
        [vm(COMPACT), vm(NX), vm(NODES), vm(NODES)], [pltpu.VMEM((1, UNK, LANES), F32)],
    )
    y_all = exchanged(y)
    states, acc, nx, ny, nz, part, base = call(
        middle_kernel,
        [nodes, keep(x), keep(y), *[keep(k) for k in (ux, uy, uz, xx, xy, xz)]],
        [vm(NODES), vm(NODES), vm(NX), vm(NODES), vm(NODES), vm((2,) + NODES), vm((2,) + COMPACT)],
    )
    first, base = call(
        third_kernel,
        [t, index, *[keep(k) for k in (states, acc, nx, ny, nz, part, base)], *y_all],
        [vm((2,) + COMPACT), vm((2,) + COMPACT)], [pltpu.VMEM((2, UNK, LANES), F32)],
    )
    [out] = call(
        fourth_kernel, [t, index, keep(base), *exchanged(first)],
        [jax.ShapeDtypeStruct((2, ELEMS, UNK), F32)],
        [pltpu.VMEM((2, UNK, LANES), F32), pltpu.VMEM((2,) + COMPACT, F32)],
    )
    return out


def solution(mesh):
    placed = (P("elem", None), P("elem", None, None), P("elem", None), P())
    return jax.shard_map(
        on_device, mesh=mesh, in_specs=placed, out_specs=P("section", "elem", None), check_vma=False
    )
```

```python
import functools
import math

import jax
import jax.numpy as jnp
from jax import lax
from jax.experimental import pallas as pl
from jax.experimental.pallas import tpu as pltpu
from jax.sharding import PartitionSpec as P

ELEMS = 32
FIELDS = 5
UNK = 320
ROWS = 80
LANES = 128
GROUPS = 10
EARLY = 3
SECTIONS = 4

time_step = 0.03
dissipation = 2.0
enthalpy_factor = 3.5
radau_nodes = [0.08858795951270394, 0.4094668644407347, 0.787659461760847, 1.0]


def lobatto():
    inner = 1.0 / math.sqrt(5.0)
    nodes = [-1.0, -inner, inner, 1.0]
    products = []
    for row in range(4):
        value = 1.0
        for other in range(4):
            if other != row:
                value = value * (nodes[row] - nodes[other])
        products.append(value)
    return [
        [
            0.0 if row == column
            else 2.0 * (products[row] / products[column]) / (nodes[row] - nodes[column])
            for column in range(4)
        ]
        for row in range(4)
    ]


def radau_table():
    columns = []
    for column in range(SECTIONS):
        coeffs = [1.0]
        scale = 1.0
        for other in range(SECTIONS):
            if other != column:
                shifted = [0.0] + coeffs
                for position in range(len(coeffs)):
                    shifted[position] = shifted[position] - radau_nodes[other] * coeffs[position]
                coeffs = shifted
                scale = scale * (radau_nodes[column] - radau_nodes[other])
        columns.append([0.0] + [c / (k + 1.0) / scale for k, c in enumerate(coeffs)])
    butcher = []
    for row in range(SECTIONS):
        entries = []
        for column in range(SECTIONS):
            value = 0.0
            for coefficient in reversed(columns[column]):
                value = value * radau_nodes[row] + coefficient
            entries.append(value)
        butcher.append(entries)
    return butcher


DERIV = lobatto()
WEIGHT = 6.0
BUTCHER = radau_table()
ROW_SUM = [sum(row) for row in BUTCHER]
COUPLING = [time_step * BUTCHER[i][i] * dissipation * WEIGHT for i in range(SECTIONS)]
STEP_X = [time_step * ROW_SUM[i] for i in range(SECTIONS)]
STEP_Y = [time_step * ROW_SUM[i] * COUPLING[i] for i in range(SECTIONS)]

ORDERS = [('ahead', 'after', 'before', 'beyond'), ('beyond', 'ahead', 'after', 'before'), ('after', 'before', 'beyond', 'ahead'), ('beyond', 'ahead', 'after', 'before')]


def sublane():
    return lax.broadcasted_iota(jnp.int32, (8, LANES), 0)


def lane():
    return lax.broadcasted_iota(jnp.int32, (8, LANES), 1)


def by_row(values):
    s = sublane()
    out = jnp.full((8, LANES), values[7], jnp.float32)
    for row in range(6, -1, -1):
        out = jnp.where(s == row, values[row], out)
    return out


def by_group(values):
    group = lane() // 32
    out = jnp.full((8, LANES), values[3], jnp.float32)
    for g in range(2, -1, -1):
        out = jnp.where(group == g, values[g], out)
    return out


def roll_rows(x, shift):
    shape = x.shape
    y = x.reshape(-1, 8, LANES)
    return pltpu.roll(y, shift % 8, axis=1).reshape(shape)


def roll_lanes(x, shift):
    if shift % LANES == 0:
        return x
    shape = x.shape
    y = x.reshape(-1, LANES)
    return pltpu.roll(y, shift % LANES, axis=1).reshape(shape)


def pick_lanes(x, index):
    shape = x.shape
    y = x.reshape(-1, LANES)
    wide = jnp.broadcast_to(index[None], (y.shape[0] // 8, 8, LANES)).reshape(y.shape)
    return jnp.take_along_axis(y, wide, axis=1, mode="promise_in_bounds").reshape(shape)


def prepared(u):
    half = [0.5 * u[f] for f in range(FIELDS)]
    square = half[1] * half[1] + half[2] * half[2] + half[3] * half[3]
    return half + [enthalpy_factor * half[4], square]


def take(state, index):
    return [x[index] for x in state]


def pair_flux(a, b, direction):
    density, v0, v1, v2, pressure, energy, square = [x + y for x, y in zip(a, b)]
    velocity = [v0, v1, v2]
    normal = velocity[direction]
    mass = density * normal
    out = [mass]
    for comp in range(3):
        momentum = mass * velocity[comp]
        out.append(momentum + pressure if comp == direction else momentum)
    out.append(normal * (energy + density * square))
    return out


def volume(u):
    n = prepared(u)
    d = DERIV
    rows = [[None] * 4 for _ in range(FIELDS)]

    def add(f, i, value):
        rows[f][i] = value if rows[f][i] is None else rows[f][i] + value

    for i in range(4):
        for other in range(i + 1, 4):
            flux = pair_flux(take(n, i), take(n, other), 0)
            for f in range(FIELDS):
                add(f, i, d[i][other] * flux[f])
                add(f, other, d[other][i] * flux[f])
    low = [(s // 4) for s in range(8)]
    c_same_low = by_row([d[j][1 - j] for j in low])
    c_same_high = by_row([d[2 + j][3 - j] for j in low])
    c_up = by_row([d[j][2 + j] for j in low])
    c_down = by_row([d[2 + j][j] for j in low])
    c_up_turn = by_row([d[j][3 - j] for j in low])
    c_down_turn = by_row([d[2 + j][1 - j] for j in low])
    c_next = [by_row([d[s % 4][(s % 4 + r) % 4] for s in range(8)]) for r in (1, 2, 3)]
    within = sublane() % 4

    def spin(x, r):
        return jnp.where(within + r < 4, roll_rows(x, 8 - r), roll_rows(x, 4 - r))

    for i in range(4):
        a = [x[i, 0] for x in n]
        b = [x[i, 1] for x in n]
        ra = [roll_rows(x, 4) for x in a]
        rb = [roll_rows(x, 4) for x in b]
        f1 = pair_flux(a, ra, 1)
        f2 = pair_flux(b, rb, 1)
        f3 = pair_flux(a, b, 1)
        f4 = pair_flux(a, rb, 1)
        f5 = pair_flux(b, ra, 1)
        n_i = [x[i] for x in n]
        z1 = pair_flux(n_i, [spin(x, 1) for x in n_i], 2)
        z2 = pair_flux(n_i, [spin(x, 2) for x in n_i], 2)
        for f in range(FIELDS):
            upper = c_same_low * f1[f] + c_up * f3[f] + c_up_turn * f4[f]
            lower = c_same_high * f2[f] + c_down * f3[f] + c_down_turn * f5[f]
            add(f, i, jnp.stack([upper, lower]))
            add(f, i, c_next[0] * z1[f] + c_next[1] * z2[f] + c_next[2] * spin(z1[f], 3))
    return jnp.stack([jnp.stack(rows[f]) for f in range(FIELDS)])


def face_terms(u, nx, ny, nz):
    n = prepared(u)
    px, py, pz = prepared(nx), prepared(ny), prepared(nz)
    half = 0.5 * dissipation
    s = sublane()
    low_x = pair_flux(take(n, 0), [x[0] for x in px], 0)
    high_x = pair_flux(take(n, 3), [x[1] for x in px], 0)
    y0 = pair_flux([x[:, 0] for x in n], [x[:, 0] for x in py], 1)
    y1 = pair_flux([x[:, 1] for x in n], [x[:, 1] for x in py], 1)
    z = pair_flux(n, pz, 2)
    k = s % 4
    sign_z = jnp.where(k == 0, -WEIGHT, WEIGHT)
    on_z = (k == 0) | (k == 3)
    out = []
    for f in range(FIELDS):
        part_z = jnp.where(on_z, sign_z * z[f] - (WEIGHT * half) * (nz[f] - u[f]), 0.0)
        part_y0 = jnp.where(s < 4, -WEIGHT * y0[f] - (WEIGHT * half) * (ny[f][:, 0] - u[f][:, 0]), 0.0)
        part_y1 = jnp.where(s < 4, 0.0, WEIGHT * y1[f] - (WEIGHT * half) * (ny[f][:, 1] - u[f][:, 1]))
        total = part_z + jnp.stack([part_y0, part_y1], axis=1)
        x0 = -WEIGHT * low_x[f] - (WEIGHT * half) * (nx[f][0] - u[f][0])
        x3 = WEIGHT * high_x[f] - (WEIGHT * half) * (nx[f][1] - u[f][3])
        out.append(jnp.stack([total[0] + x0, total[1], total[2], total[3] + x3]))
    return jnp.stack(out)


def lifted(nx, ny, nz):
    s = sublane()
    k = s % 4
    y = jnp.stack([jnp.where(s < 4, ny[:, :, 0], 0.0), jnp.where(s < 4, 0.0, ny[:, :, 1])], axis=2)
    total = y + jnp.where((k == 0) | (k == 3), nz, 0.0)
    return jnp.stack([total[:, 0] + nx[:, 0], total[:, 1], total[:, 2], total[:, 3] + nx[:, 1]], axis=1)


def aligned(near, far, index):
    nx = jnp.stack([pick_lanes(near[:, 3], index[0]), pick_lanes(near[:, 0], index[1])], axis=1)
    ny = jnp.stack(
        [
            roll_rows(pick_lanes(near[:, :, 1], index[2]), 4),
            roll_rows(pick_lanes(near[:, :, 0], index[3]), 4),
        ],
        axis=2,
    )
    lower = roll_rows(pick_lanes(near, index[4]), 5)
    upper = roll_rows(pick_lanes(far, index[5]), 3)
    nz = jnp.where(sublane() % 4 == 0, lower, upper)
    return nx, ny, nz


def nodes_of(parts):
    return jnp.stack([p.reshape(FIELDS, 2, 8, LANES) for p in parts], axis=1)


def group_of(x, groups):
    at = lane()[:1] // 32
    parts = [roll_lanes(y, 32 * (g - group)) for g, (y, group) in enumerate(zip(x, groups))]
    out = parts[-1]
    for g in range(len(parts) - 2, -1, -1):
        out = jnp.where(at == g, parts[g], out)
    return out


def near_far(own, before, after, ahead, beyond):
    near = nodes_of([group_of([before, own, after], [i] * 3) for i in range(4)])
    far = nodes_of([group_of([ahead, beyond], [i] * 2) for i in range(4)])
    return near, far


def spread(compact):
    base = lane() % 32
    return nodes_of([pick_lanes(compact, base + 32 * i) for i in range(4)])


def squeezed(nodes):
    at = lane() // 32
    parts = [nodes[:, i].reshape(ROWS // 8, 8, LANES) for i in range(4)]
    out = parts[3]
    for i in range(2, -1, -1):
        out = jnp.where(at == i, parts[i], out)
    return out.reshape(ROWS, LANES)


def flipped(x):
    pieces = [
        x[:, 0:128].T,
        x[:, 128:256].T,
        jnp.concatenate([x[:, 256:320], jnp.zeros((LANES, 64), jnp.float32)], axis=1).T[:64],
    ]
    return jnp.concatenate(pieces, axis=0).reshape(FIELDS, 4, 2, 8, LANES)


def multiply(t_ref, v_ref, out_ref, count, finish):
    def block(g, carry):
        rows = pl.ds(pl.multiple_of(g * 8, 8), 8)
        sums = [jnp.zeros((8, 8, LANES), jnp.float32) for _ in range(count)]
        for q in range(UNK // 8):
            piece = t_ref[rows, 8 * q : 8 * q + 8, :]
            for c in range(count):
                sums[c] = sums[c] + piece * v_ref[c, 8 * q : 8 * q + 8, :][None]
        for c in range(count):
            finish(c, rows, jnp.sum(sums[c], axis=1))
        return carry

    lax.fori_loop(0, GROUPS, block, 0)


def prepare_kernel(inv_ref, neighbours_ref, partners_ref, u_ref, t_ref, index_ref, nodes_ref, acc_ref,
                   wide, tail, square, line_ref, own, sems, small):
    smalls = [
        pltpu.make_async_copy(u_ref, own, small.at[0]),
        pltpu.make_async_copy(neighbours_ref, square, small.at[1]),
        pltpu.make_async_copy(partners_ref, line_ref, small.at[2]),
    ]
    for copy in smalls:
        copy.start()

    def pieces(g, i, start):
        rows = pl.ds(start, 8)
        return [
            pltpu.make_async_copy(inv_ref.at[:, rows, pl.ds(0, 128)], wide.at[g, 0, i], sems.at[g, i, 0]),
            pltpu.make_async_copy(inv_ref.at[:, rows, pl.ds(128, 128)], wide.at[g, 1, i], sems.at[g, i, 1]),
            pltpu.make_async_copy(inv_ref.at[:, rows, pl.ds(256, 64)], tail.at[g, i], sems.at[g, i, 2]),
        ]

    for g in range(GROUPS):
        f, half = g // 2, g % 2
        for i in range(4):
            for copy in pieces(g, i, f * 64 + i * 16 + half * 8):
                copy.start()
    def turn_group(g, carry):
        for i in range(4):
            for copy in pieces(g, i, 0):
                copy.wait()
        for r in range(8):
            rows = pl.ds(r, LANES, stride=8)
            t_ref[g * 8 + r, 0:128] = wide.at[g, 0].reshape(1024, LANES)[rows, :].T
            t_ref[g * 8 + r, 128:256] = wide.at[g, 1].reshape(1024, LANES)[rows, :].T
            t_ref[g * 8 + r, 256:320] = tail[g, :, :, r, :].reshape(LANES, 64).T
        return carry

    lax.fori_loop(0, EARLY, turn_group, 0)
    for copy in smalls:
        copy.wait()
    count = lax.axis_size("elem")
    rank = lax.axis_index("elem")
    base = lane() % 32
    turned = jnp.concatenate([square[...]] * 4, axis=1)

    def slots(values, first):
        block = lax.shift_right_logical(values, 5) - rank - first
        block = jnp.where(block < 0, block + count, block)
        block = jnp.where(block < 0, block + count, block)
        block = jnp.where(block >= count, block - count, block)
        return block * ELEMS + (values & 31)

    near = slots(turned, -1)
    for face in range(5):
        index_ref[face] = jnp.broadcast_to(near[face : face + 1], (8, LANES))
    line = jnp.broadcast_to(line_ref[pl.ds(rank // 4, 1), :], (8, LANES))
    line = jnp.take_along_axis(line, base + (rank % 4) * 32, axis=1, mode="promise_in_bounds")
    index_ref[5] = slots(line, count // 4)
    u = flipped(jnp.concatenate([own[...]] * 4, axis=0))
    nodes_ref[...] = u
    acc_ref[...] = volume(u)
    lax.fori_loop(EARLY, GROUPS, turn_group, 0)


def first_kernel(t_ref, index_ref, nodes_ref, acc_ref, moved,
                 x_ref, nx_ref, ny_ref, nz_ref, v_ref):
    before, after, ahead, beyond = pulled(moved)
    near = flipped(jnp.concatenate([before, before, after, after], axis=0))
    near = jnp.where(lane() // 32 == 1, nodes_ref[...], near)
    far = flipped(jnp.concatenate([ahead, beyond] * 2, axis=0))
    nx, ny, nz = aligned(near, far, index_ref[...])
    nx_ref[...], ny_ref[...], nz_ref[...] = nx, ny, nz
    total = acc_ref[...] + face_terms(nodes_ref[...], nx, ny, nz)
    v_ref[0] = (-2.0 * total).reshape(UNK, LANES)

    def finish(c, rows, value):
        x_ref[rows, :] = value

    multiply(t_ref, v_ref, x_ref, 1, finish)


def second_kernel(t_ref, index_ref, own_ref, moved,
                  y_ref, nx_ref, ny_ref, nz_ref, v_ref):
    near, far = near_far(own_ref[...], *pulled(moved))
    nx, ny, nz = aligned(near, far, index_ref[...])
    nx_ref[...], ny_ref[...], nz_ref[...] = nx, ny, nz
    v_ref[0] = lifted(nx, ny, nz).reshape(UNK, LANES)

    def finish(c, rows, value):
        y_ref[rows, :] = value

    multiply(t_ref, v_ref, y_ref, 1, finish)


def section_value(table, which):
    first = lax.axis_index("section") == 0
    return jnp.where(first, table[which], table[2 + which]).astype(jnp.float32)


def middle_kernel(u_ref, x_ref, y_ref, ux_ref, uy_ref, uz_ref, xx_ref, xy_ref, xz_ref,
                  states_ref, acc_ref, nx_ref, ny_ref, nz_ref, part_ref, base_ref):
    u = u_ref[...]
    x, y = spread(x_ref[...]), spread(y_ref[...])
    a = by_group(STEP_X)
    states = u + a * x + by_group(STEP_Y) * y
    states_ref[...] = states
    acc_ref[...] = volume(states)
    nx_ref[...] = ux_ref[...] + a * xx_ref[...]
    ny_ref[...] = uy_ref[...] + a * xy_ref[...]
    nz_ref[...] = uz_ref[...] + a * xz_ref[...]
    compact = squeezed(u)
    for c in range(2):
        part_ref[c] = -section_value(STEP_X, c) * x - section_value(STEP_Y, c) * y
        base_ref[c] = compact + section_value(STEP_X, c) * x_ref[...] + section_value(STEP_Y, c) * y_ref[...]


def third_kernel(t_ref, index_ref, states_ref, acc_ref, nx_ref, ny_ref, nz_ref, part_ref, base_ref,
                 own_ref, moved, first_ref, sum_ref, v_ref):
    near, far = near_far(own_ref[...], *pulled(moved))
    yx, yy, yz = aligned(near, far, index_ref[...])
    b = by_group(STEP_Y)
    total = acc_ref[...] + face_terms(
        states_ref[...], nx_ref[...] + b * yx, ny_ref[...] + b * yy, nz_ref[...] + b * yz
    )
    turned = [total] + [roll_lanes(total, 32 * r) for r in (1, 2, 3)]
    for c in range(2):
        v = part_ref[c]
        for r in range(4):
            factor = by_group(
                [
                    section_value([-2.0 * time_step * BUTCHER[s][(g - r) % 4] for s in range(4)], c)
                    for g in range(4)
                ]
            )
            v = v + factor * turned[r]
        v_ref[c] = v.reshape(UNK, LANES)

    def finish(c, rows, value):
        first_ref[c, rows, :] = value
        sum_ref[c, rows, :] = base_ref[c, rows, :] + value

    multiply(t_ref, v_ref, first_ref, 2, finish)


def fourth_kernel(t_ref, index_ref, base_ref, own_ref, moved, out_ref, v_ref, done_ref):
    for c in range(2):
        near, far = near_far(own_ref[c], *pulled(moved, c))
        v_ref[c] = lifted(*aligned(near, far, index_ref[...])).reshape(UNK, LANES)

    def finish(c, rows, value):
        done_ref[c, rows, :] = base_ref[c, rows, :] + section_value(COUPLING, c) * value

    multiply(t_ref, v_ref, done_ref, 2, finish)
    both = nodes_of([group_of([done_ref[0], done_ref[1]], [i] * 2) for i in range(4)]).reshape(UNK, LANES)
    turned = [
        both[0:128].T,
        both[128:256].T,
        jnp.concatenate([both[256:320], both[256:320]], axis=0).T[:, :64],
    ]
    for c in range(2):
        rows = slice(c * ELEMS, (c + 1) * ELEMS)
        out_ref[c, :, 0:128] = turned[0][rows]
        out_ref[c, :, 128:256] = turned[1][rows]
        out_ref[c, :, 256:320] = turned[2][rows]


VMEM = pltpu.VMEM
F32 = jnp.float32
NODES = (FIELDS, 4, 2, 8, LANES)
NX = (FIELDS, 2, 2, 8, LANES)
COMPACT = (ROWS, LANES)


def call(kernel, inputs, outputs, scratch=(), anywhere=(), flops=10**7, room=8):
    in_specs = [pl.BlockSpec(memory_space=pltpu.HBM if i in anywhere else VMEM) for i in range(len(inputs))]
    return pl.pallas_call(
        kernel,
        out_shape=outputs,
        in_specs=in_specs,
        out_specs=[pl.BlockSpec(memory_space=VMEM)] * len(outputs),
        scratch_shapes=list(scratch),
        compiler_params=pltpu.CompilerParams(vmem_limit_bytes=room * 2**20),
        cost_estimate=pl.CostEstimate(flops=flops, bytes_accessed=10**6, transcendentals=0),
    )(*inputs)


def vm(shape, dtype=F32):
    return pltpu.VMEM(shape, dtype)


def routes(count):
    far = count // 4
    return {
        "before": [(i - 1) % count for i in range(count)],
        "after": [(i + 1) % count for i in range(count)],
        "inner": [i ^ 1 for i in range(count)],
        "outer": [(i - 1 + 2 * (i % 2)) % count for i in range(count)],
        "ahead": [(i + far) % count for i in range(count)],
        "beyond": [(i + far + 1) % count for i in range(count)],
    }


def pulled(moved, at=Ellipsis):
    got = {name: ref[at] for name, ref in moved.items()}
    if "inner" in got:
        odd = lax.axis_index("elem") % 2 == 1
        got["before"] = jnp.where(odd, got["inner"], got["outer"])
        got["after"] = jnp.where(odd, got["outer"], got["inner"])
    return got["before"], got["after"], got["ahead"], got["beyond"]


def exchanged(block, order):
    table = routes(lax.axis_size("elem"))
    return {name: lax.ppermute(block, "elem", [(s, i) for i, s in enumerate(table[name])]) for name in order}


def with_moved(kernel, inputs, moved, outputs, scratch):
    count = len(inputs)
    names = list(moved)

    def whole(*refs):
        kernel(*refs[:count], dict(zip(names, refs[count:])), *refs[count + len(names) :])

    return call(whole, [*inputs, *moved.values()], outputs, scratch)


def keep(x):
    return pltpu.with_memory_space_constraint(x, VMEM)


def on_device(u_start, inverses, neighbours, partners):
    partners = partners.reshape(-1, LANES)
    u_moved = exchanged(u_start, ORDERS[0])
    t, index, nodes, acc = call(
        prepare_kernel,
        [pltpu.with_memory_space_constraint(k, pltpu.HBM) for k in (inverses, neighbours.T, partners, u_start)],
        [vm((ROWS, UNK, LANES)), vm((6, 8, LANES), jnp.int32), vm(NODES), vm(NODES)],
        [
            pltpu.VMEM((GROUPS, 2, 4, ELEMS, 8, LANES), F32),
            pltpu.VMEM((GROUPS, 4, ELEMS, 8, 64), F32),
            pltpu.VMEM((5, ELEMS), jnp.int32),
            pltpu.VMEM((partners.shape[0], LANES), jnp.int32),
            pltpu.VMEM((ELEMS, UNK), F32),
            pltpu.SemaphoreType.DMA((GROUPS, 4, 3)),
            pltpu.SemaphoreType.DMA((3,)),
        ],
        anywhere=(0, 1, 2, 3),
        flops=10**9,
        room=24,
    )
    t, index, nodes = keep(t), keep(index), keep(nodes)
    single = [pltpu.VMEM((1, UNK, LANES), F32)]
    faces = [vm(COMPACT), vm(NX), vm(NODES), vm(NODES)]
    x, ux, uy, uz = with_moved(first_kernel, [t, index, nodes, keep(acc)], u_moved, faces, single)
    y, xx, xy, xz = with_moved(second_kernel, [t, index, x], exchanged(x, ORDERS[1]), faces, single)
    y_moved = exchanged(y, ORDERS[2])
    states, acc, nx, ny, nz, part, base = call(
        middle_kernel,
        [nodes, keep(x), keep(y), *[keep(k) for k in (ux, uy, uz, xx, xy, xz)]],
        [vm(NODES), vm(NODES), vm(NX), vm(NODES), vm(NODES), vm((2,) + NODES), vm((2,) + COMPACT)],
    )
    first, base = with_moved(
        third_kernel,
        [t, index, *[keep(k) for k in (states, acc, nx, ny, nz, part, base)], y],
        y_moved,
        [vm((2,) + COMPACT), vm((2,) + COMPACT)],
        [pltpu.VMEM((2, UNK, LANES), F32)],
    )
    [out] = with_moved(
        fourth_kernel,
        [t, index, keep(base), first],
        exchanged(first, ORDERS[3]),
        [jax.ShapeDtypeStruct((2, ELEMS, UNK), F32)],
        [pltpu.VMEM((2, UNK, LANES), F32), pltpu.VMEM((2,) + COMPACT, F32)],
    )
    return out


def solution(mesh):
    placed = (P("elem", None), P("elem", None, None), P("elem", None), P())
    return jax.shard_map(
        on_device, mesh=mesh, in_specs=placed, out_specs=P("section", "elem", None), check_vma=False
    )
```

```python
import functools
import math

import jax
import jax.numpy as jnp
from jax import lax
from jax.experimental import pallas as pl
from jax.experimental.pallas import tpu as pltpu
from jax.sharding import PartitionSpec as P

ELEMS = 32
FIELDS = 5
UNK = 320
ROWS = 80
LANES = 128
GROUPS = 10
SECTIONS = 4

time_step = 0.03
dissipation = 2.0
enthalpy_factor = 3.5
radau_nodes = [0.08858795951270394, 0.4094668644407347, 0.787659461760847, 1.0]


def lobatto():
    inner = 1.0 / math.sqrt(5.0)
    nodes = [-1.0, -inner, inner, 1.0]
    products = []
    for row in range(4):
        value = 1.0
        for other in range(4):
            if other != row:
                value = value * (nodes[row] - nodes[other])
        products.append(value)
    return [
        [
            0.0 if row == column
            else 2.0 * (products[row] / products[column]) / (nodes[row] - nodes[column])
            for column in range(4)
        ]
        for row in range(4)
    ]


def radau_table():
    columns = []
    for column in range(SECTIONS):
        coeffs = [1.0]
        scale = 1.0
        for other in range(SECTIONS):
            if other != column:
                shifted = [0.0] + coeffs
                for position in range(len(coeffs)):
                    shifted[position] = shifted[position] - radau_nodes[other] * coeffs[position]
                coeffs = shifted
                scale = scale * (radau_nodes[column] - radau_nodes[other])
        columns.append([0.0] + [c / (k + 1.0) / scale for k, c in enumerate(coeffs)])
    butcher = []
    for row in range(SECTIONS):
        entries = []
        for column in range(SECTIONS):
            value = 0.0
            for coefficient in reversed(columns[column]):
                value = value * radau_nodes[row] + coefficient
            entries.append(value)
        butcher.append(entries)
    return butcher


DERIV = lobatto()
WEIGHT = 6.0
BUTCHER = radau_table()
ROW_SUM = [sum(row) for row in BUTCHER]
COUPLING = [time_step * BUTCHER[i][i] * dissipation * WEIGHT for i in range(SECTIONS)]
STEP_X = [time_step * ROW_SUM[i] for i in range(SECTIONS)]
STEP_Y = [time_step * ROW_SUM[i] * COUPLING[i] for i in range(SECTIONS)]

ORDERS = [('ahead', 'after', 'before', 'beyond'), ('beyond', 'ahead', 'after', 'before'), ('after', 'before', 'beyond', 'ahead'), ('beyond', 'ahead', 'after', 'before')]


def sublane():
    return lax.broadcasted_iota(jnp.int32, (8, LANES), 0)


def lane():
    return lax.broadcasted_iota(jnp.int32, (8, LANES), 1)


def by_row(values):
    s = sublane()
    out = jnp.full((8, LANES), values[7], jnp.float32)
    for row in range(6, -1, -1):
        out = jnp.where(s == row, values[row], out)
    return out


def by_group(values):
    group = lane() // 32
    out = jnp.full((8, LANES), values[3], jnp.float32)
    for g in range(2, -1, -1):
        out = jnp.where(group == g, values[g], out)
    return out


def roll_rows(x, shift):
    shape = x.shape
    y = x.reshape(-1, 8, LANES)
    return pltpu.roll(y, shift % 8, axis=1).reshape(shape)


def roll_lanes(x, shift):
    if shift % LANES == 0:
        return x
    shape = x.shape
    y = x.reshape(-1, LANES)
    return pltpu.roll(y, shift % LANES, axis=1).reshape(shape)


def pick_lanes(x, index):
    shape = x.shape
    y = x.reshape(-1, LANES)
    wide = jnp.broadcast_to(index[None], (y.shape[0] // 8, 8, LANES)).reshape(y.shape)
    return jnp.take_along_axis(y, wide, axis=1, mode="promise_in_bounds").reshape(shape)


def prepared(u):
    half = [0.5 * u[f] for f in range(FIELDS)]
    square = half[1] * half[1] + half[2] * half[2] + half[3] * half[3]
    return half + [enthalpy_factor * half[4], square]


def take(state, index):
    return [x[index] for x in state]


def pair_flux(a, b, direction):
    density, v0, v1, v2, pressure, energy, square = [x + y for x, y in zip(a, b)]
    velocity = [v0, v1, v2]
    normal = velocity[direction]
    mass = density * normal
    out = [mass]
    for comp in range(3):
        momentum = mass * velocity[comp]
        out.append(momentum + pressure if comp == direction else momentum)
    out.append(normal * (energy + density * square))
    return out


def volume(u):
    n = prepared(u)
    d = DERIV
    rows = [[None] * 4 for _ in range(FIELDS)]

    def add(f, i, value):
        rows[f][i] = value if rows[f][i] is None else rows[f][i] + value

    for i in range(4):
        for other in range(i + 1, 4):
            flux = pair_flux(take(n, i), take(n, other), 0)
            for f in range(FIELDS):
                add(f, i, d[i][other] * flux[f])
                add(f, other, d[other][i] * flux[f])
    low = [(s // 4) for s in range(8)]
    c_same_low = by_row([d[j][1 - j] for j in low])
    c_same_high = by_row([d[2 + j][3 - j] for j in low])
    c_up = by_row([d[j][2 + j] for j in low])
    c_down = by_row([d[2 + j][j] for j in low])
    c_up_turn = by_row([d[j][3 - j] for j in low])
    c_down_turn = by_row([d[2 + j][1 - j] for j in low])
    c_next = [by_row([d[s % 4][(s % 4 + r) % 4] for s in range(8)]) for r in (1, 2, 3)]
    within = sublane() % 4

    def spin(x, r):
        return jnp.where(within + r < 4, roll_rows(x, 8 - r), roll_rows(x, 4 - r))

    for i in range(4):
        a = [x[i, 0] for x in n]
        b = [x[i, 1] for x in n]
        ra = [roll_rows(x, 4) for x in a]
        rb = [roll_rows(x, 4) for x in b]
        f1 = pair_flux(a, ra, 1)
        f2 = pair_flux(b, rb, 1)
        f3 = pair_flux(a, b, 1)
        f4 = pair_flux(a, rb, 1)
        f5 = pair_flux(b, ra, 1)
        n_i = [x[i] for x in n]
        z1 = pair_flux(n_i, [spin(x, 1) for x in n_i], 2)
        z2 = pair_flux(n_i, [spin(x, 2) for x in n_i], 2)
        for f in range(FIELDS):
            upper = c_same_low * f1[f] + c_up * f3[f] + c_up_turn * f4[f]
            lower = c_same_high * f2[f] + c_down * f3[f] + c_down_turn * f5[f]
            add(f, i, jnp.stack([upper, lower]))
            add(f, i, c_next[0] * z1[f] + c_next[1] * z2[f] + c_next[2] * spin(z1[f], 3))
    return jnp.stack([jnp.stack(rows[f]) for f in range(FIELDS)])


def face_terms(u, nx, ny, nz):
    n = prepared(u)
    px, py, pz = prepared(nx), prepared(ny), prepared(nz)
    half = 0.5 * dissipation
    s = sublane()
    low_x = pair_flux(take(n, 0), [x[0] for x in px], 0)
    high_x = pair_flux(take(n, 3), [x[1] for x in px], 0)
    y0 = pair_flux([x[:, 0] for x in n], [x[:, 0] for x in py], 1)
    y1 = pair_flux([x[:, 1] for x in n], [x[:, 1] for x in py], 1)
    z = pair_flux(n, pz, 2)
    k = s % 4
    sign_z = jnp.where(k == 0, -WEIGHT, WEIGHT)
    on_z = (k == 0) | (k == 3)
    out = []
    for f in range(FIELDS):
        part_z = jnp.where(on_z, sign_z * z[f] - (WEIGHT * half) * (nz[f] - u[f]), 0.0)
        part_y0 = jnp.where(s < 4, -WEIGHT * y0[f] - (WEIGHT * half) * (ny[f][:, 0] - u[f][:, 0]), 0.0)
        part_y1 = jnp.where(s < 4, 0.0, WEIGHT * y1[f] - (WEIGHT * half) * (ny[f][:, 1] - u[f][:, 1]))
        total = part_z + jnp.stack([part_y0, part_y1], axis=1)
        x0 = -WEIGHT * low_x[f] - (WEIGHT * half) * (nx[f][0] - u[f][0])
        x3 = WEIGHT * high_x[f] - (WEIGHT * half) * (nx[f][1] - u[f][3])
        out.append(jnp.stack([total[0] + x0, total[1], total[2], total[3] + x3]))
    return jnp.stack(out)


def lifted(nx, ny, nz):
    s = sublane()
    k = s % 4
    y = jnp.stack([jnp.where(s < 4, ny[:, :, 0], 0.0), jnp.where(s < 4, 0.0, ny[:, :, 1])], axis=2)
    total = y + jnp.where((k == 0) | (k == 3), nz, 0.0)
    return jnp.stack([total[:, 0] + nx[:, 0], total[:, 1], total[:, 2], total[:, 3] + nx[:, 1]], axis=1)


def aligned(near, far, index):
    nx = jnp.stack([pick_lanes(near[:, 3], index[0]), pick_lanes(near[:, 0], index[1])], axis=1)
    ny = jnp.stack(
        [
            roll_rows(pick_lanes(near[:, :, 1], index[2]), 4),
            roll_rows(pick_lanes(near[:, :, 0], index[3]), 4),
        ],
        axis=2,
    )
    lower = roll_rows(pick_lanes(near, index[4]), 5)
    upper = roll_rows(pick_lanes(far, index[5]), 3)
    nz = jnp.where(sublane() % 4 == 0, lower, upper)
    return nx, ny, nz


def nodes_of(parts):
    return jnp.stack([p.reshape(FIELDS, 2, 8, LANES) for p in parts], axis=1)


def group_of(x, groups):
    at = lane()[:1] // 32
    parts = [roll_lanes(y, 32 * (g - group)) for g, (y, group) in enumerate(zip(x, groups))]
    out = parts[-1]
    for g in range(len(parts) - 2, -1, -1):
        out = jnp.where(at == g, parts[g], out)
    return out


def near_far(own, before, after, ahead, beyond):
    near = nodes_of([group_of([before, own, after], [i] * 3) for i in range(4)])
    far = nodes_of([group_of([ahead, beyond], [i] * 2) for i in range(4)])
    return near, far


def spread(compact):
    base = lane() % 32
    return nodes_of([pick_lanes(compact, base + 32 * i) for i in range(4)])


def squeezed(nodes):
    at = lane() // 32
    parts = [nodes[:, i].reshape(ROWS // 8, 8, LANES) for i in range(4)]
    out = parts[3]
    for i in range(2, -1, -1):
        out = jnp.where(at == i, parts[i], out)
    return out.reshape(ROWS, LANES)


def flipped(x):
    pieces = [
        x[:, 0:128].T,
        x[:, 128:256].T,
        jnp.concatenate([x[:, 256:320], jnp.zeros((LANES, 64), jnp.float32)], axis=1).T[:64],
    ]
    return jnp.concatenate(pieces, axis=0).reshape(FIELDS, 4, 2, 8, LANES)


def multiply(t_ref, v_ref, out_ref, count, finish):
    def block(g, carry):
        rows = pl.ds(pl.multiple_of(g * 8, 8), 8)
        sums = [jnp.zeros((8, 8, LANES), jnp.float32) for _ in range(count)]
        for q in range(UNK // 8):
            piece = t_ref[rows, 8 * q : 8 * q + 8, :]
            for c in range(count):
                sums[c] = sums[c] + piece * v_ref[c, 8 * q : 8 * q + 8, :][None]
        for c in range(count):
            finish(c, rows, jnp.sum(sums[c], axis=1))
        return carry

    lax.fori_loop(0, GROUPS, block, 0)


def prepare_kernel(inv_ref, neighbours_ref, partners_ref, u_ref, t_ref, index_ref, nodes_ref, acc_ref,
                   wide, tail, square, line_ref, own, sems, small):
    smalls = [
        pltpu.make_async_copy(u_ref, own, small.at[0]),
        pltpu.make_async_copy(neighbours_ref, square, small.at[1]),
        pltpu.make_async_copy(partners_ref, line_ref, small.at[2]),
    ]
    for copy in smalls:
        copy.start()

    def pieces(g, i, start):
        rows = pl.ds(start, 8)
        return [
            pltpu.make_async_copy(inv_ref.at[:, rows, pl.ds(0, 128)], wide.at[g, 0, i], sems.at[g, i, 0]),
            pltpu.make_async_copy(inv_ref.at[:, rows, pl.ds(128, 128)], wide.at[g, 1, i], sems.at[g, i, 1]),
            pltpu.make_async_copy(inv_ref.at[:, rows, pl.ds(256, 64)], tail.at[g, i], sems.at[g, i, 2]),
        ]

    for g in range(GROUPS):
        f, half = g // 2, g % 2
        for i in range(4):
            for copy in pieces(g, i, f * 64 + i * 16 + half * 8):
                copy.start()
    def turn_group(g, carry):
        for i in range(4):
            for copy in pieces(g, i, 0):
                copy.wait()
        for r in range(8):
            rows = pl.ds(r, LANES, stride=8)
            t_ref[g * 8 + r, 0:128] = wide.at[g, 0].reshape(1024, LANES)[rows, :].T
            t_ref[g * 8 + r, 128:256] = wide.at[g, 1].reshape(1024, LANES)[rows, :].T
            t_ref[g * 8 + r, 256:320] = tail[g, :, :, r, :].reshape(LANES, 64).T
        return carry

    lax.fori_loop(0, GROUPS, turn_group, 0)
    for copy in smalls:
        copy.wait()
    count = lax.axis_size("elem")
    rank = lax.axis_index("elem")
    base = lane() % 32
    turned = jnp.concatenate([square[...]] * 4, axis=1)

    def slots(values, first):
        block = lax.shift_right_logical(values, 5) - rank - first
        block = jnp.where(block < 0, block + count, block)
        block = jnp.where(block < 0, block + count, block)
        block = jnp.where(block >= count, block - count, block)
        return block * ELEMS + (values & 31)

    near = slots(turned, -1)
    for face in range(5):
        index_ref[face] = jnp.broadcast_to(near[face : face + 1], (8, LANES))
    line = jnp.broadcast_to(line_ref[pl.ds(rank // 4, 1), :], (8, LANES))
    line = jnp.take_along_axis(line, base + (rank % 4) * 32, axis=1, mode="promise_in_bounds")
    index_ref[5] = slots(line, count // 4)
    u = flipped(jnp.concatenate([own[...]] * 4, axis=0))
    nodes_ref[...] = u
    acc_ref[...] = volume(u)


def first_kernel(t_ref, index_ref, nodes_ref, acc_ref, moved,
                 x_ref, nx_ref, ny_ref, nz_ref, v_ref):
    before, after, ahead, beyond = pulled(moved)
    near = flipped(jnp.concatenate([before, before, after, after], axis=0))
    near = jnp.where(lane() // 32 == 1, nodes_ref[...], near)
    far = flipped(jnp.concatenate([ahead, beyond] * 2, axis=0))
    nx, ny, nz = aligned(near, far, index_ref[...])
    nx_ref[...], ny_ref[...], nz_ref[...] = nx, ny, nz
    total = acc_ref[...] + face_terms(nodes_ref[...], nx, ny, nz)
    v_ref[0] = (-2.0 * total).reshape(UNK, LANES)

    def finish(c, rows, value):
        x_ref[rows, :] = value

    multiply(t_ref, v_ref, x_ref, 1, finish)


def second_kernel(t_ref, index_ref, own_ref, moved,
                  y_ref, nx_ref, ny_ref, nz_ref, v_ref):
    near, far = near_far(own_ref[...], *pulled(moved))
    nx, ny, nz = aligned(near, far, index_ref[...])
    nx_ref[...], ny_ref[...], nz_ref[...] = nx, ny, nz
    v_ref[0] = lifted(nx, ny, nz).reshape(UNK, LANES)

    def finish(c, rows, value):
        y_ref[rows, :] = value

    multiply(t_ref, v_ref, y_ref, 1, finish)


def section_value(table, which):
    first = lax.axis_index("section") == 0
    return jnp.where(first, table[which], table[2 + which]).astype(jnp.float32)


def middle_kernel(u_ref, x_ref, y_ref, ux_ref, uy_ref, uz_ref, xx_ref, xy_ref, xz_ref,
                  states_ref, acc_ref, nx_ref, ny_ref, nz_ref, part_ref, base_ref):
    u = u_ref[...]
    x, y = spread(x_ref[...]), spread(y_ref[...])
    a = by_group(STEP_X)
    states = u + a * x + by_group(STEP_Y) * y
    states_ref[...] = states
    acc_ref[...] = volume(states)
    nx_ref[...] = ux_ref[...] + a * xx_ref[...]
    ny_ref[...] = uy_ref[...] + a * xy_ref[...]
    nz_ref[...] = uz_ref[...] + a * xz_ref[...]
    compact = squeezed(u)
    for c in range(2):
        part_ref[c] = -section_value(STEP_X, c) * x - section_value(STEP_Y, c) * y
        base_ref[c] = compact + section_value(STEP_X, c) * x_ref[...] + section_value(STEP_Y, c) * y_ref[...]


def third_kernel(t_ref, index_ref, states_ref, acc_ref, nx_ref, ny_ref, nz_ref, part_ref, base_ref,
                 own_ref, moved, first_ref, sum_ref, v_ref):
    near, far = near_far(own_ref[...], *pulled(moved))
    yx, yy, yz = aligned(near, far, index_ref[...])
    b = by_group(STEP_Y)
    total = acc_ref[...] + face_terms(
        states_ref[...], nx_ref[...] + b * yx, ny_ref[...] + b * yy, nz_ref[...] + b * yz
    )
    turned = [total] + [roll_lanes(total, 32 * r) for r in (1, 2, 3)]
    for c in range(2):
        v = part_ref[c]
        for r in range(4):
            factor = by_group(
                [
                    section_value([-2.0 * time_step * BUTCHER[s][(g - r) % 4] for s in range(4)], c)
                    for g in range(4)
                ]
            )
            v = v + factor * turned[r]
        v_ref[c] = v.reshape(UNK, LANES)

    def finish(c, rows, value):
        first_ref[c, rows, :] = value
        sum_ref[c, rows, :] = base_ref[c, rows, :] + value

    multiply(t_ref, v_ref, first_ref, 2, finish)


def fourth_kernel(t_ref, index_ref, base_ref, own_ref, moved, out_ref, v_ref, done_ref):
    for c in range(2):
        near, far = near_far(own_ref[c], *pulled(moved, c))
        v_ref[c] = lifted(*aligned(near, far, index_ref[...])).reshape(UNK, LANES)

    def finish(c, rows, value):
        done_ref[c, rows, :] = base_ref[c, rows, :] + section_value(COUPLING, c) * value

    multiply(t_ref, v_ref, done_ref, 2, finish)
    both = nodes_of([group_of([done_ref[0], done_ref[1]], [i] * 2) for i in range(4)]).reshape(UNK, LANES)
    turned = [
        both[0:128].T,
        both[128:256].T,
        jnp.concatenate([both[256:320], both[256:320]], axis=0).T[:, :64],
    ]
    for c in range(2):
        rows = slice(c * ELEMS, (c + 1) * ELEMS)
        out_ref[c, :, 0:128] = turned[0][rows]
        out_ref[c, :, 128:256] = turned[1][rows]
        out_ref[c, :, 256:320] = turned[2][rows]


VMEM = pltpu.VMEM
F32 = jnp.float32
NODES = (FIELDS, 4, 2, 8, LANES)
NX = (FIELDS, 2, 2, 8, LANES)
COMPACT = (ROWS, LANES)


def call(kernel, inputs, outputs, scratch=(), anywhere=(), flops=10**7, room=8):
    in_specs = [pl.BlockSpec(memory_space=pltpu.HBM if i in anywhere else VMEM) for i in range(len(inputs))]
    return pl.pallas_call(
        kernel,
        out_shape=outputs,
        in_specs=in_specs,
        out_specs=[pl.BlockSpec(memory_space=VMEM)] * len(outputs),
        scratch_shapes=list(scratch),
        compiler_params=pltpu.CompilerParams(vmem_limit_bytes=room * 2**20),
        cost_estimate=pl.CostEstimate(flops=flops, bytes_accessed=10**6, transcendentals=0),
    )(*inputs)


def vm(shape, dtype=F32):
    return pltpu.VMEM(shape, dtype)


def routes(count):
    far = count // 4
    return {
        "before": [(i - 1) % count for i in range(count)],
        "after": [(i + 1) % count for i in range(count)],
        "inner": [i ^ 1 for i in range(count)],
        "outer": [(i - 1 + 2 * (i % 2)) % count for i in range(count)],
        "ahead": [(i + far) % count for i in range(count)],
        "beyond": [(i + far + 1) % count for i in range(count)],
    }


def pulled(moved, at=Ellipsis):
    got = {name: ref[at] for name, ref in moved.items()}
    if "inner" in got:
        odd = lax.axis_index("elem") % 2 == 1
        got["before"] = jnp.where(odd, got["inner"], got["outer"])
        got["after"] = jnp.where(odd, got["outer"], got["inner"])
    return got["before"], got["after"], got["ahead"], got["beyond"]


def exchanged(block, order):
    table = routes(lax.axis_size("elem"))
    return {name: lax.ppermute(block, "elem", [(s, i) for i, s in enumerate(table[name])]) for name in order}


def with_moved(kernel, inputs, moved, outputs, scratch):
    count = len(inputs)
    names = list(moved)

    def whole(*refs):
        kernel(*refs[:count], dict(zip(names, refs[count:])), *refs[count + len(names) :])

    return call(whole, [*inputs, *moved.values()], outputs, scratch)


def keep(x):
    return pltpu.with_memory_space_constraint(x, VMEM)


def on_device(u_start, inverses, neighbours, partners):
    partners = partners.reshape(-1, LANES)
    u_moved = exchanged(u_start, ORDERS[0])
    t, index, nodes, acc = call(
        prepare_kernel,
        [pltpu.with_memory_space_constraint(k, pltpu.HBM) for k in (inverses, neighbours.T, partners, u_start)],
        [vm((ROWS, UNK, LANES)), vm((6, 8, LANES), jnp.int32), vm(NODES), vm(NODES)],
        [
            pltpu.VMEM((GROUPS, 2, 4, ELEMS, 8, LANES), F32),
            pltpu.VMEM((GROUPS, 4, ELEMS, 8, 64), F32),
            pltpu.VMEM((5, ELEMS), jnp.int32),
            pltpu.VMEM((partners.shape[0], LANES), jnp.int32),
            pltpu.VMEM((ELEMS, UNK), F32),
            pltpu.SemaphoreType.DMA((GROUPS, 4, 3)),
            pltpu.SemaphoreType.DMA((3,)),
        ],
        anywhere=(0, 1, 2, 3),
        flops=10**9,
        room=24,
    )
    t, index, nodes = keep(t), keep(index), keep(nodes)
    single = [pltpu.VMEM((1, UNK, LANES), F32)]
    faces = [vm(COMPACT), vm(NX), vm(NODES), vm(NODES)]
    x, ux, uy, uz = with_moved(first_kernel, [t, index, nodes, keep(acc)], u_moved, faces, single)
    y, xx, xy, xz = with_moved(second_kernel, [t, index, x], exchanged(x, ORDERS[1]), faces, single)
    y_moved = exchanged(y, ORDERS[2])
    states, acc, nx, ny, nz, part, base = call(
        middle_kernel,
        [nodes, keep(x), keep(y), *[keep(k) for k in (ux, uy, uz, xx, xy, xz)]],
        [vm(NODES), vm(NODES), vm(NX), vm(NODES), vm(NODES), vm((2,) + NODES), vm((2,) + COMPACT)],
    )
    first, base = with_moved(
        third_kernel,
        [t, index, *[keep(k) for k in (states, acc, nx, ny, nz, part, base)], y],
        y_moved,
        [vm((2,) + COMPACT), vm((2,) + COMPACT)],
        [pltpu.VMEM((2, UNK, LANES), F32)],
    )
    [out] = with_moved(
        fourth_kernel,
        [t, index, keep(base), first],
        exchanged(first, ORDERS[3]),
        [jax.ShapeDtypeStruct((2, ELEMS, UNK), F32)],
        [pltpu.VMEM((2, UNK, LANES), F32), pltpu.VMEM((2,) + COMPACT, F32)],
    )
    return out


def solution(mesh):
    placed = (P("elem", None), P("elem", None, None), P("elem", None), P())
    return jax.shard_map(
        on_device, mesh=mesh, in_specs=placed, out_specs=P("section", "elem", None), check_vma=False
    )
```

```python
import functools
import math

import jax
import jax.numpy as jnp
from jax import lax
from jax.experimental import pallas as pl
from jax.experimental.pallas import tpu as pltpu
from jax.sharding import PartitionSpec as P

ELEMS = 32
FIELDS = 5
UNK = 320
ROWS = 80
LANES = 128
GROUPS = 10
SECTIONS = 4

time_step = 0.03
dissipation = 2.0
enthalpy_factor = 3.5
radau_nodes = [0.08858795951270394, 0.4094668644407347, 0.787659461760847, 1.0]


def lobatto():
    inner = 1.0 / math.sqrt(5.0)
    nodes = [-1.0, -inner, inner, 1.0]
    products = []
    for row in range(4):
        value = 1.0
        for other in range(4):
            if other != row:
                value = value * (nodes[row] - nodes[other])
        products.append(value)
    return [
        [
            0.0 if row == column
            else 2.0 * (products[row] / products[column]) / (nodes[row] - nodes[column])
            for column in range(4)
        ]
        for row in range(4)
    ]


def radau_table():
    columns = []
    for column in range(SECTIONS):
        coeffs = [1.0]
        scale = 1.0
        for other in range(SECTIONS):
            if other != column:
                shifted = [0.0] + coeffs
                for position in range(len(coeffs)):
                    shifted[position] = shifted[position] - radau_nodes[other] * coeffs[position]
                coeffs = shifted
                scale = scale * (radau_nodes[column] - radau_nodes[other])
        columns.append([0.0] + [c / (k + 1.0) / scale for k, c in enumerate(coeffs)])
    butcher = []
    for row in range(SECTIONS):
        entries = []
        for column in range(SECTIONS):
            value = 0.0
            for coefficient in reversed(columns[column]):
                value = value * radau_nodes[row] + coefficient
            entries.append(value)
        butcher.append(entries)
    return butcher


DERIV = lobatto()
WEIGHT = 6.0
BUTCHER = radau_table()
ROW_SUM = [sum(row) for row in BUTCHER]
COUPLING = [time_step * BUTCHER[i][i] * dissipation * WEIGHT for i in range(SECTIONS)]
STEP_X = [time_step * ROW_SUM[i] for i in range(SECTIONS)]
STEP_Y = [time_step * ROW_SUM[i] * COUPLING[i] for i in range(SECTIONS)]

ORDERS = [('before', 'ahead', 'after', 'beyond'), ('beyond', 'ahead', 'after', 'before'), ('after', 'before', 'beyond', 'ahead'), ('beyond', 'ahead', 'after', 'before')]


def sublane():
    return lax.broadcasted_iota(jnp.int32, (8, LANES), 0)


def lane():
    return lax.broadcasted_iota(jnp.int32, (8, LANES), 1)


def by_row(values):
    s = sublane()
    out = jnp.full((8, LANES), values[7], jnp.float32)
    for row in range(6, -1, -1):
        out = jnp.where(s == row, values[row], out)
    return out


def by_group(values):
    group = lane() // 32
    out = jnp.full((8, LANES), values[3], jnp.float32)
    for g in range(2, -1, -1):
        out = jnp.where(group == g, values[g], out)
    return out


def roll_rows(x, shift):
    shape = x.shape
    y = x.reshape(-1, 8, LANES)
    return pltpu.roll(y, shift % 8, axis=1).reshape(shape)


def roll_lanes(x, shift):
    if shift % LANES == 0:
        return x
    shape = x.shape
    y = x.reshape(-1, LANES)
    return pltpu.roll(y, shift % LANES, axis=1).reshape(shape)


def pick_lanes(x, index):
    shape = x.shape
    y = x.reshape(-1, LANES)
    wide = jnp.broadcast_to(index[None], (y.shape[0] // 8, 8, LANES)).reshape(y.shape)
    return jnp.take_along_axis(y, wide, axis=1, mode="promise_in_bounds").reshape(shape)


def prepared(u):
    half = [0.5 * u[f] for f in range(FIELDS)]
    square = half[1] * half[1] + half[2] * half[2] + half[3] * half[3]
    return half + [enthalpy_factor * half[4], square]


def take(state, index):
    return [x[index] for x in state]


def pair_flux(a, b, direction):
    density, v0, v1, v2, pressure, energy, square = [x + y for x, y in zip(a, b)]
    velocity = [v0, v1, v2]
    normal = velocity[direction]
    mass = density * normal
    out = [mass]
    for comp in range(3):
        momentum = mass * velocity[comp]
        out.append(momentum + pressure if comp == direction else momentum)
    out.append(normal * (energy + density * square))
    return out


def volume(u):
    n = prepared(u)
    d = DERIV
    rows = [[None] * 4 for _ in range(FIELDS)]

    def add(f, i, value):
        rows[f][i] = value if rows[f][i] is None else rows[f][i] + value

    for i in range(4):
        for other in range(i + 1, 4):
            flux = pair_flux(take(n, i), take(n, other), 0)
            for f in range(FIELDS):
                add(f, i, d[i][other] * flux[f])
                add(f, other, d[other][i] * flux[f])
    low = [(s // 4) for s in range(8)]
    c_same_low = by_row([d[j][1 - j] for j in low])
    c_same_high = by_row([d[2 + j][3 - j] for j in low])
    c_up = by_row([d[j][2 + j] for j in low])
    c_down = by_row([d[2 + j][j] for j in low])
    c_up_turn = by_row([d[j][3 - j] for j in low])
    c_down_turn = by_row([d[2 + j][1 - j] for j in low])
    c_next = [by_row([d[s % 4][(s % 4 + r) % 4] for s in range(8)]) for r in (1, 2, 3)]
    within = sublane() % 4

    def spin(x, r):
        return jnp.where(within + r < 4, roll_rows(x, 8 - r), roll_rows(x, 4 - r))

    for i in range(4):
        a = [x[i, 0] for x in n]
        b = [x[i, 1] for x in n]
        ra = [roll_rows(x, 4) for x in a]
        rb = [roll_rows(x, 4) for x in b]
        f1 = pair_flux(a, ra, 1)
        f2 = pair_flux(b, rb, 1)
        f3 = pair_flux(a, b, 1)
        f4 = pair_flux(a, rb, 1)
        f5 = pair_flux(b, ra, 1)
        n_i = [x[i] for x in n]
        z1 = pair_flux(n_i, [spin(x, 1) for x in n_i], 2)
        z2 = pair_flux(n_i, [spin(x, 2) for x in n_i], 2)
        for f in range(FIELDS):
            upper = c_same_low * f1[f] + c_up * f3[f] + c_up_turn * f4[f]
            lower = c_same_high * f2[f] + c_down * f3[f] + c_down_turn * f5[f]
            add(f, i, jnp.stack([upper, lower]))
            add(f, i, c_next[0] * z1[f] + c_next[1] * z2[f] + c_next[2] * spin(z1[f], 3))
    return jnp.stack([jnp.stack(rows[f]) for f in range(FIELDS)])


def face_terms(u, nx, ny, nz):
    n = prepared(u)
    px, py, pz = prepared(nx), prepared(ny), prepared(nz)
    half = 0.5 * dissipation
    s = sublane()
    low_x = pair_flux(take(n, 0), [x[0] for x in px], 0)
    high_x = pair_flux(take(n, 3), [x[1] for x in px], 0)
    y0 = pair_flux([x[:, 0] for x in n], [x[:, 0] for x in py], 1)
    y1 = pair_flux([x[:, 1] for x in n], [x[:, 1] for x in py], 1)
    z = pair_flux(n, pz, 2)
    k = s % 4
    sign_z = jnp.where(k == 0, -WEIGHT, WEIGHT)
    on_z = (k == 0) | (k == 3)
    out = []
    for f in range(FIELDS):
        part_z = jnp.where(on_z, sign_z * z[f] - (WEIGHT * half) * (nz[f] - u[f]), 0.0)
        part_y0 = jnp.where(s < 4, -WEIGHT * y0[f] - (WEIGHT * half) * (ny[f][:, 0] - u[f][:, 0]), 0.0)
        part_y1 = jnp.where(s < 4, 0.0, WEIGHT * y1[f] - (WEIGHT * half) * (ny[f][:, 1] - u[f][:, 1]))
        total = part_z + jnp.stack([part_y0, part_y1], axis=1)
        x0 = -WEIGHT * low_x[f] - (WEIGHT * half) * (nx[f][0] - u[f][0])
        x3 = WEIGHT * high_x[f] - (WEIGHT * half) * (nx[f][1] - u[f][3])
        out.append(jnp.stack([total[0] + x0, total[1], total[2], total[3] + x3]))
    return jnp.stack(out)


def lifted(nx, ny, nz):
    s = sublane()
    k = s % 4
    y = jnp.stack([jnp.where(s < 4, ny[:, :, 0], 0.0), jnp.where(s < 4, 0.0, ny[:, :, 1])], axis=2)
    total = y + jnp.where((k == 0) | (k == 3), nz, 0.0)
    return jnp.stack([total[:, 0] + nx[:, 0], total[:, 1], total[:, 2], total[:, 3] + nx[:, 1]], axis=1)


def aligned(near, far, index):
    nx = jnp.stack([pick_lanes(near[:, 3], index[0]), pick_lanes(near[:, 0], index[1])], axis=1)
    ny = jnp.stack(
        [
            roll_rows(pick_lanes(near[:, :, 1], index[2]), 4),
            roll_rows(pick_lanes(near[:, :, 0], index[3]), 4),
        ],
        axis=2,
    )
    lower = roll_rows(pick_lanes(near, index[4]), 5)
    upper = roll_rows(pick_lanes(far, index[5]), 3)
    nz = jnp.where(sublane() % 4 == 0, lower, upper)
    return nx, ny, nz


def nodes_of(parts):
    return jnp.stack([p.reshape(FIELDS, 2, 8, LANES) for p in parts], axis=1)


def group_of(x, groups):
    at = lane()[:1] // 32
    parts = [roll_lanes(y, 32 * (g - group)) for g, (y, group) in enumerate(zip(x, groups))]
    out = parts[-1]
    for g in range(len(parts) - 2, -1, -1):
        out = jnp.where(at == g, parts[g], out)
    return out


def near_far(own, before, after, ahead, beyond):
    near = nodes_of([group_of([before, own, after], [i] * 3) for i in range(4)])
    far = nodes_of([group_of([ahead, beyond], [i] * 2) for i in range(4)])
    return near, far


def spread(compact):
    base = lane() % 32
    return nodes_of([pick_lanes(compact, base + 32 * i) for i in range(4)])


def squeezed(nodes):
    at = lane() // 32
    parts = [nodes[:, i].reshape(ROWS // 8, 8, LANES) for i in range(4)]
    out = parts[3]
    for i in range(2, -1, -1):
        out = jnp.where(at == i, parts[i], out)
    return out.reshape(ROWS, LANES)


def flipped(x):
    pieces = [
        x[:, 0:128].T,
        x[:, 128:256].T,
        jnp.concatenate([x[:, 256:320], jnp.zeros((LANES, 64), jnp.float32)], axis=1).T[:64],
    ]
    return jnp.concatenate(pieces, axis=0).reshape(FIELDS, 4, 2, 8, LANES)


def multiply(t_ref, v_ref, out_ref, count, finish):
    def block(g, carry):
        rows = pl.ds(pl.multiple_of(g * 8, 8), 8)
        sums = [jnp.zeros((8, 8, LANES), jnp.float32) for _ in range(count)]
        for q in range(UNK // 8):
            piece = t_ref[rows, 8 * q : 8 * q + 8, :]
            for c in range(count):
                sums[c] = sums[c] + piece * v_ref[c, 8 * q : 8 * q + 8, :][None]
        for c in range(count):
            finish(c, rows, jnp.sum(sums[c], axis=1))
        return carry

    lax.fori_loop(0, GROUPS, block, 0)


def prepare_kernel(inv_ref, neighbours_ref, partners_ref, u_ref, t_ref, index_ref, nodes_ref, acc_ref,
                   wide, tail, square, line_ref, own, sems, small):
    smalls = [
        pltpu.make_async_copy(u_ref, own, small.at[0]),
        pltpu.make_async_copy(neighbours_ref, square, small.at[1]),
        pltpu.make_async_copy(partners_ref, line_ref, small.at[2]),
    ]
    for copy in smalls:
        copy.start()

    def pieces(g, i, start):
        rows = pl.ds(start, 8)
        return [
            pltpu.make_async_copy(inv_ref.at[:, rows, pl.ds(0, 128)], wide.at[g, 0, i], sems.at[g, i, 0]),
            pltpu.make_async_copy(inv_ref.at[:, rows, pl.ds(128, 128)], wide.at[g, 1, i], sems.at[g, i, 1]),
            pltpu.make_async_copy(inv_ref.at[:, rows, pl.ds(256, 64)], tail.at[g, i], sems.at[g, i, 2]),
        ]

    for g in range(GROUPS):
        f, half = g // 2, g % 2
        for i in range(4):
            for copy in pieces(g, i, f * 64 + i * 16 + half * 8):
                copy.start()
    def turn_group(g, carry):
        for i in range(4):
            for copy in pieces(g, i, 0):
                copy.wait()
        for r in range(8):
            rows = pl.ds(r, LANES, stride=8)
            t_ref[g * 8 + r, 0:128] = wide.at[g, 0].reshape(1024, LANES)[rows, :].T
            t_ref[g * 8 + r, 128:256] = wide.at[g, 1].reshape(1024, LANES)[rows, :].T
            t_ref[g * 8 + r, 256:320] = tail[g, :, :, r, :].reshape(LANES, 64).T
        return carry

    lax.fori_loop(0, GROUPS, turn_group, 0)
    for copy in smalls:
        copy.wait()
    count = lax.axis_size("elem")
    rank = lax.axis_index("elem")
    base = lane() % 32
    turned = jnp.concatenate([square[...]] * 4, axis=1)

    def slots(values, first):
        block = lax.shift_right_logical(values, 5) - rank - first
        block = jnp.where(block < 0, block + count, block)
        block = jnp.where(block < 0, block + count, block)
        block = jnp.where(block >= count, block - count, block)
        return block * ELEMS + (values & 31)

    near = slots(turned, -1)
    for face in range(5):
        index_ref[face] = jnp.broadcast_to(near[face : face + 1], (8, LANES))
    line = jnp.broadcast_to(line_ref[pl.ds(rank // 4, 1), :], (8, LANES))
    line = jnp.take_along_axis(line, base + (rank % 4) * 32, axis=1, mode="promise_in_bounds")
    index_ref[5] = slots(line, count // 4)
    u = flipped(jnp.concatenate([own[...]] * 4, axis=0))
    nodes_ref[...] = u
    acc_ref[...] = volume(u)


def first_kernel(t_ref, index_ref, nodes_ref, acc_ref, moved,
                 x_ref, nx_ref, ny_ref, nz_ref, v_ref):
    before, after, ahead, beyond = pulled(moved)
    near = flipped(jnp.concatenate([before, before, after, after], axis=0))
    near = jnp.where(lane() // 32 == 1, nodes_ref[...], near)
    far = flipped(jnp.concatenate([ahead, beyond] * 2, axis=0))
    nx, ny, nz = aligned(near, far, index_ref[...])
    nx_ref[...], ny_ref[...], nz_ref[...] = nx, ny, nz
    total = acc_ref[...] + face_terms(nodes_ref[...], nx, ny, nz)
    v_ref[0] = (-2.0 * total).reshape(UNK, LANES)

    def finish(c, rows, value):
        x_ref[rows, :] = value

    multiply(t_ref, v_ref, x_ref, 1, finish)


def second_kernel(t_ref, index_ref, own_ref, moved,
                  y_ref, nx_ref, ny_ref, nz_ref, v_ref):
    near, far = near_far(own_ref[...], *pulled(moved))
    nx, ny, nz = aligned(near, far, index_ref[...])
    nx_ref[...], ny_ref[...], nz_ref[...] = nx, ny, nz
    v_ref[0] = lifted(nx, ny, nz).reshape(UNK, LANES)

    def finish(c, rows, value):
        y_ref[rows, :] = value

    multiply(t_ref, v_ref, y_ref, 1, finish)


def section_value(table, which):
    first = lax.axis_index("section") == 0
    return jnp.where(first, table[which], table[2 + which]).astype(jnp.float32)


def middle_kernel(u_ref, x_ref, y_ref, ux_ref, uy_ref, uz_ref, xx_ref, xy_ref, xz_ref,
                  states_ref, acc_ref, nx_ref, ny_ref, nz_ref, part_ref, base_ref):
    u = u_ref[...]
    x, y = spread(x_ref[...]), spread(y_ref[...])
    a = by_group(STEP_X)
    states = u + a * x + by_group(STEP_Y) * y
    states_ref[...] = states
    acc_ref[...] = volume(states)
    nx_ref[...] = ux_ref[...] + a * xx_ref[...]
    ny_ref[...] = uy_ref[...] + a * xy_ref[...]
    nz_ref[...] = uz_ref[...] + a * xz_ref[...]
    compact = squeezed(u)
    for c in range(2):
        part_ref[c] = -section_value(STEP_X, c) * x - section_value(STEP_Y, c) * y
        base_ref[c] = compact + section_value(STEP_X, c) * x_ref[...] + section_value(STEP_Y, c) * y_ref[...]


def third_kernel(t_ref, index_ref, states_ref, acc_ref, nx_ref, ny_ref, nz_ref, part_ref, base_ref,
                 own_ref, moved, first_ref, sum_ref, v_ref):
    near, far = near_far(own_ref[...], *pulled(moved))
    yx, yy, yz = aligned(near, far, index_ref[...])
    b = by_group(STEP_Y)
    total = acc_ref[...] + face_terms(
        states_ref[...], nx_ref[...] + b * yx, ny_ref[...] + b * yy, nz_ref[...] + b * yz
    )
    turned = [total] + [roll_lanes(total, 32 * r) for r in (1, 2, 3)]
    for c in range(2):
        v = part_ref[c]
        for r in range(4):
            factor = by_group(
                [
                    section_value([-2.0 * time_step * BUTCHER[s][(g - r) % 4] for s in range(4)], c)
                    for g in range(4)
                ]
            )
            v = v + factor * turned[r]
        v_ref[c] = v.reshape(UNK, LANES)

    def finish(c, rows, value):
        first_ref[c, rows, :] = value
        sum_ref[c, rows, :] = base_ref[c, rows, :] + value

    multiply(t_ref, v_ref, first_ref, 2, finish)


def fourth_kernel(t_ref, index_ref, base_ref, own_ref, moved, out_ref, v_ref, done_ref):
    for c in range(2):
        near, far = near_far(own_ref[c], *pulled(moved, c))
        v_ref[c] = lifted(*aligned(near, far, index_ref[...])).reshape(UNK, LANES)

    def finish(c, rows, value):
        done_ref[c, rows, :] = base_ref[c, rows, :] + section_value(COUPLING, c) * value

    multiply(t_ref, v_ref, done_ref, 2, finish)
    both = nodes_of([group_of([done_ref[0], done_ref[1]], [i] * 2) for i in range(4)]).reshape(UNK, LANES)
    turned = [
        both[0:128].T,
        both[128:256].T,
        jnp.concatenate([both[256:320], both[256:320]], axis=0).T[:, :64],
    ]
    for c in range(2):
        rows = slice(c * ELEMS, (c + 1) * ELEMS)
        out_ref[c, :, 0:128] = turned[0][rows]
        out_ref[c, :, 128:256] = turned[1][rows]
        out_ref[c, :, 256:320] = turned[2][rows]


VMEM = pltpu.VMEM
F32 = jnp.float32
NODES = (FIELDS, 4, 2, 8, LANES)
NX = (FIELDS, 2, 2, 8, LANES)
COMPACT = (ROWS, LANES)


def call(kernel, inputs, outputs, scratch=(), anywhere=(), flops=10**7, room=8):
    in_specs = [pl.BlockSpec(memory_space=pltpu.HBM if i in anywhere else VMEM) for i in range(len(inputs))]
    return pl.pallas_call(
        kernel,
        out_shape=outputs,
        in_specs=in_specs,
        out_specs=[pl.BlockSpec(memory_space=VMEM)] * len(outputs),
        scratch_shapes=list(scratch),
        compiler_params=pltpu.CompilerParams(vmem_limit_bytes=room * 2**20),
        cost_estimate=pl.CostEstimate(flops=flops, bytes_accessed=10**6, transcendentals=0),
    )(*inputs)


def vm(shape, dtype=F32):
    return pltpu.VMEM(shape, dtype)


def routes(count):
    far = count // 4
    return {
        "before": [(i - 1) % count for i in range(count)],
        "after": [(i + 1) % count for i in range(count)],
        "inner": [i ^ 1 for i in range(count)],
        "outer": [(i - 1 + 2 * (i % 2)) % count for i in range(count)],
        "ahead": [(i + far) % count for i in range(count)],
        "beyond": [(i + far + 1) % count for i in range(count)],
    }


def pulled(moved, at=Ellipsis):
    got = {name: ref[at] for name, ref in moved.items()}
    if "inner" in got:
        odd = lax.axis_index("elem") % 2 == 1
        got["before"] = jnp.where(odd, got["inner"], got["outer"])
        got["after"] = jnp.where(odd, got["outer"], got["inner"])
    return got["before"], got["after"], got["ahead"], got["beyond"]


def exchanged(block, order):
    table = routes(lax.axis_size("elem"))
    return {name: lax.ppermute(block, "elem", [(s, i) for i, s in enumerate(table[name])]) for name in order}


def with_moved(kernel, inputs, moved, outputs, scratch):
    count = len(inputs)
    names = list(moved)

    def whole(*refs):
        kernel(*refs[:count], dict(zip(names, refs[count:])), *refs[count + len(names) :])

    return call(whole, [*inputs, *moved.values()], outputs, scratch)


def keep(x):
    return pltpu.with_memory_space_constraint(x, VMEM)


def on_device(u_start, inverses, neighbours, partners):
    partners = partners.reshape(-1, LANES)
    u_moved = exchanged(u_start, ORDERS[0])
    t, index, nodes, acc = call(
        prepare_kernel,
        [pltpu.with_memory_space_constraint(k, pltpu.HBM) for k in (inverses, neighbours.T, partners, u_start)],
        [vm((ROWS, UNK, LANES)), vm((6, 8, LANES), jnp.int32), vm(NODES), vm(NODES)],
        [
            pltpu.VMEM((GROUPS, 2, 4, ELEMS, 8, LANES), F32),
            pltpu.VMEM((GROUPS, 4, ELEMS, 8, 64), F32),
            pltpu.VMEM((5, ELEMS), jnp.int32),
            pltpu.VMEM((partners.shape[0], LANES), jnp.int32),
            pltpu.VMEM((ELEMS, UNK), F32),
            pltpu.SemaphoreType.DMA((GROUPS, 4, 3)),
            pltpu.SemaphoreType.DMA((3,)),
        ],
        anywhere=(0, 1, 2, 3),
        flops=10**9,
        room=24,
    )
    t, index, nodes = keep(t), keep(index), keep(nodes)
    single = [pltpu.VMEM((1, UNK, LANES), F32)]
    faces = [vm(COMPACT), vm(NX), vm(NODES), vm(NODES)]
    x, ux, uy, uz = with_moved(first_kernel, [t, index, nodes, keep(acc)], u_moved, faces, single)
    y, xx, xy, xz = with_moved(second_kernel, [t, index, x], exchanged(x, ORDERS[1]), faces, single)
    y_moved = exchanged(y, ORDERS[2])
    states, acc, nx, ny, nz, part, base = call(
        middle_kernel,
        [nodes, keep(x), keep(y), *[keep(k) for k in (ux, uy, uz, xx, xy, xz)]],
        [vm(NODES), vm(NODES), vm(NX), vm(NODES), vm(NODES), vm((2,) + NODES), vm((2,) + COMPACT)],
    )
    first, base = with_moved(
        third_kernel,
        [t, index, *[keep(k) for k in (states, acc, nx, ny, nz, part, base)], y],
        y_moved,
        [vm((2,) + COMPACT), vm((2,) + COMPACT)],
        [pltpu.VMEM((2, UNK, LANES), F32)],
    )
    [out] = with_moved(
        fourth_kernel,
        [t, index, keep(base), first],
        exchanged(first, ORDERS[3]),
        [jax.ShapeDtypeStruct((2, ELEMS, UNK), F32)],
        [pltpu.VMEM((2, UNK, LANES), F32), pltpu.VMEM((2,) + COMPACT, F32)],
    )
    return out


def solution(mesh):
    placed = (P("elem", None), P("elem", None, None), P("elem", None), P())
    return jax.shard_map(
        on_device, mesh=mesh, in_specs=placed, out_specs=P("section", "elem", None), check_vma=False
    )
```

```python
import functools
import math

import jax
import jax.numpy as jnp
from jax import lax
from jax.experimental import pallas as pl
from jax.experimental.pallas import tpu as pltpu
from jax.sharding import PartitionSpec as P

ELEMS = 32
FIELDS = 5
UNK = 320
ROWS = 80
LANES = 128
GROUPS = 10
SECTIONS = 4

time_step = 0.03
dissipation = 2.0
enthalpy_factor = 3.5
radau_nodes = [0.08858795951270394, 0.4094668644407347, 0.787659461760847, 1.0]


def lobatto():
    inner = 1.0 / math.sqrt(5.0)
    nodes = [-1.0, -inner, inner, 1.0]
    products = []
    for row in range(4):
        value = 1.0
        for other in range(4):
            if other != row:
                value = value * (nodes[row] - nodes[other])
        products.append(value)
    return [
        [
            0.0 if row == column
            else 2.0 * (products[row] / products[column]) / (nodes[row] - nodes[column])
            for column in range(4)
        ]
        for row in range(4)
    ]


def radau_table():
    columns = []
    for column in range(SECTIONS):
        coeffs = [1.0]
        scale = 1.0
        for other in range(SECTIONS):
            if other != column:
                shifted = [0.0] + coeffs
                for position in range(len(coeffs)):
                    shifted[position] = shifted[position] - radau_nodes[other] * coeffs[position]
                coeffs = shifted
                scale = scale * (radau_nodes[column] - radau_nodes[other])
        columns.append([0.0] + [c / (k + 1.0) / scale for k, c in enumerate(coeffs)])
    butcher = []
    for row in range(SECTIONS):
        entries = []
        for column in range(SECTIONS):
            value = 0.0
            for coefficient in reversed(columns[column]):
                value = value * radau_nodes[row] + coefficient
            entries.append(value)
        butcher.append(entries)
    return butcher


DERIV = lobatto()
WEIGHT = 6.0
BUTCHER = radau_table()
ROW_SUM = [sum(row) for row in BUTCHER]
COUPLING = [time_step * BUTCHER[i][i] * dissipation * WEIGHT for i in range(SECTIONS)]
STEP_X = [time_step * ROW_SUM[i] for i in range(SECTIONS)]
STEP_Y = [time_step * ROW_SUM[i] * COUPLING[i] for i in range(SECTIONS)]

ORDERS = [('before', 'ahead', 'after', 'beyond'), ('beyond', 'ahead', 'after', 'before'), ('after', 'before', 'beyond', 'ahead'), ('ahead', 'beyond', 'after', 'before')]


def sublane():
    return lax.broadcasted_iota(jnp.int32, (8, LANES), 0)


def lane():
    return lax.broadcasted_iota(jnp.int32, (8, LANES), 1)


def by_row(values):
    s = sublane()
    out = jnp.full((8, LANES), values[7], jnp.float32)
    for row in range(6, -1, -1):
        out = jnp.where(s == row, values[row], out)
    return out


def by_group(values):
    group = lane() // 32
    out = jnp.full((8, LANES), values[3], jnp.float32)
    for g in range(2, -1, -1):
        out = jnp.where(group == g, values[g], out)
    return out


def roll_rows(x, shift):
    shape = x.shape
    y = x.reshape(-1, 8, LANES)
    return pltpu.roll(y, shift % 8, axis=1).reshape(shape)


def roll_lanes(x, shift):
    if shift % LANES == 0:
        return x
    shape = x.shape
    y = x.reshape(-1, LANES)
    return pltpu.roll(y, shift % LANES, axis=1).reshape(shape)


def pick_lanes(x, index):
    shape = x.shape
    y = x.reshape(-1, LANES)
    wide = jnp.broadcast_to(index[None], (y.shape[0] // 8, 8, LANES)).reshape(y.shape)
    return jnp.take_along_axis(y, wide, axis=1, mode="promise_in_bounds").reshape(shape)


def prepared(u):
    half = [0.5 * u[f] for f in range(FIELDS)]
    square = half[1] * half[1] + half[2] * half[2] + half[3] * half[3]
    return half + [enthalpy_factor * half[4], square]


def take(state, index):
    return [x[index] for x in state]


def pair_flux(a, b, direction):
    density, v0, v1, v2, pressure, energy, square = [x + y for x, y in zip(a, b)]
    velocity = [v0, v1, v2]
    normal = velocity[direction]
    mass = density * normal
    out = [mass]
    for comp in range(3):
        momentum = mass * velocity[comp]
        out.append(momentum + pressure if comp == direction else momentum)
    out.append(normal * (energy + density * square))
    return out


def volume(u):
    n = prepared(u)
    d = DERIV
    rows = [[None] * 4 for _ in range(FIELDS)]

    def add(f, i, value):
        rows[f][i] = value if rows[f][i] is None else rows[f][i] + value

    for i in range(4):
        for other in range(i + 1, 4):
            flux = pair_flux(take(n, i), take(n, other), 0)
            for f in range(FIELDS):
                add(f, i, d[i][other] * flux[f])
                add(f, other, d[other][i] * flux[f])
    low = [(s // 4) for s in range(8)]
    c_same_low = by_row([d[j][1 - j] for j in low])
    c_same_high = by_row([d[2 + j][3 - j] for j in low])
    c_up = by_row([d[j][2 + j] for j in low])
    c_down = by_row([d[2 + j][j] for j in low])
    c_up_turn = by_row([d[j][3 - j] for j in low])
    c_down_turn = by_row([d[2 + j][1 - j] for j in low])
    c_next = [by_row([d[s % 4][(s % 4 + r) % 4] for s in range(8)]) for r in (1, 2, 3)]
    within = sublane() % 4

    def spin(x, r):
        return jnp.where(within + r < 4, roll_rows(x, 8 - r), roll_rows(x, 4 - r))

    for i in range(4):
        a = [x[i, 0] for x in n]
        b = [x[i, 1] for x in n]
        ra = [roll_rows(x, 4) for x in a]
        rb = [roll_rows(x, 4) for x in b]
        f1 = pair_flux(a, ra, 1)
        f2 = pair_flux(b, rb, 1)
        f3 = pair_flux(a, b, 1)
        f4 = pair_flux(a, rb, 1)
        f5 = pair_flux(b, ra, 1)
        n_i = [x[i] for x in n]
        z1 = pair_flux(n_i, [spin(x, 1) for x in n_i], 2)
        z2 = pair_flux(n_i, [spin(x, 2) for x in n_i], 2)
        for f in range(FIELDS):
            upper = c_same_low * f1[f] + c_up * f3[f] + c_up_turn * f4[f]
            lower = c_same_high * f2[f] + c_down * f3[f] + c_down_turn * f5[f]
            add(f, i, jnp.stack([upper, lower]))
            add(f, i, c_next[0] * z1[f] + c_next[1] * z2[f] + c_next[2] * spin(z1[f], 3))
    return jnp.stack([jnp.stack(rows[f]) for f in range(FIELDS)])


def face_terms(u, nx, ny, nz):
    n = prepared(u)
    px, py, pz = prepared(nx), prepared(ny), prepared(nz)
    half = 0.5 * dissipation
    s = sublane()
    low_x = pair_flux(take(n, 0), [x[0] for x in px], 0)
    high_x = pair_flux(take(n, 3), [x[1] for x in px], 0)
    y0 = pair_flux([x[:, 0] for x in n], [x[:, 0] for x in py], 1)
    y1 = pair_flux([x[:, 1] for x in n], [x[:, 1] for x in py], 1)
    z = pair_flux(n, pz, 2)
    k = s % 4
    sign_z = jnp.where(k == 0, -WEIGHT, WEIGHT)
    on_z = (k == 0) | (k == 3)
    out = []
    for f in range(FIELDS):
        part_z = jnp.where(on_z, sign_z * z[f] - (WEIGHT * half) * (nz[f] - u[f]), 0.0)
        part_y0 = jnp.where(s < 4, -WEIGHT * y0[f] - (WEIGHT * half) * (ny[f][:, 0] - u[f][:, 0]), 0.0)
        part_y1 = jnp.where(s < 4, 0.0, WEIGHT * y1[f] - (WEIGHT * half) * (ny[f][:, 1] - u[f][:, 1]))
        total = part_z + jnp.stack([part_y0, part_y1], axis=1)
        x0 = -WEIGHT * low_x[f] - (WEIGHT * half) * (nx[f][0] - u[f][0])
        x3 = WEIGHT * high_x[f] - (WEIGHT * half) * (nx[f][1] - u[f][3])
        out.append(jnp.stack([total[0] + x0, total[1], total[2], total[3] + x3]))
    return jnp.stack(out)


def lifted(nx, ny, nz):
    s = sublane()
    k = s % 4
    y = jnp.stack([jnp.where(s < 4, ny[:, :, 0], 0.0), jnp.where(s < 4, 0.0, ny[:, :, 1])], axis=2)
    total = y + jnp.where((k == 0) | (k == 3), nz, 0.0)
    return jnp.stack([total[:, 0] + nx[:, 0], total[:, 1], total[:, 2], total[:, 3] + nx[:, 1]], axis=1)


def aligned(near, far, index):
    nx = jnp.stack([pick_lanes(near[:, 3], index[0]), pick_lanes(near[:, 0], index[1])], axis=1)
    ny = jnp.stack(
        [
            roll_rows(pick_lanes(near[:, :, 1], index[2]), 4),
            roll_rows(pick_lanes(near[:, :, 0], index[3]), 4),
        ],
        axis=2,
    )
    lower = roll_rows(pick_lanes(near, index[4]), 5)
    upper = roll_rows(pick_lanes(far, index[5]), 3)
    nz = jnp.where(sublane() % 4 == 0, lower, upper)
    return nx, ny, nz


def nodes_of(parts):
    return jnp.stack([p.reshape(FIELDS, 2, 8, LANES) for p in parts], axis=1)


def group_of(x, groups):
    at = lane()[:1] // 32
    parts = [roll_lanes(y, 32 * (g - group)) for g, (y, group) in enumerate(zip(x, groups))]
    out = parts[-1]
    for g in range(len(parts) - 2, -1, -1):
        out = jnp.where(at == g, parts[g], out)
    return out


def near_far(own, before, after, ahead, beyond):
    near = nodes_of([group_of([before, own, after], [i] * 3) for i in range(4)])
    far = nodes_of([group_of([ahead, beyond], [i] * 2) for i in range(4)])
    return near, far


def spread(compact):
    base = lane() % 32
    return nodes_of([pick_lanes(compact, base + 32 * i) for i in range(4)])


def squeezed(nodes):
    at = lane() // 32
    parts = [nodes[:, i].reshape(ROWS // 8, 8, LANES) for i in range(4)]
    out = parts[3]
    for i in range(2, -1, -1):
        out = jnp.where(at == i, parts[i], out)
    return out.reshape(ROWS, LANES)


def flipped(x):
    pieces = [
        x[:, 0:128].T,
        x[:, 128:256].T,
        jnp.concatenate([x[:, 256:320], jnp.zeros((LANES, 64), jnp.float32)], axis=1).T[:64],
    ]
    return jnp.concatenate(pieces, axis=0).reshape(FIELDS, 4, 2, 8, LANES)


def multiply(t_ref, v_ref, out_ref, count, finish):
    def block(g, carry):
        rows = pl.ds(pl.multiple_of(g * 8, 8), 8)
        sums = [jnp.zeros((8, 8, LANES), jnp.float32) for _ in range(count)]
        for q in range(UNK // 8):
            piece = t_ref[rows, 8 * q : 8 * q + 8, :]
            for c in range(count):
                sums[c] = sums[c] + piece * v_ref[c, 8 * q : 8 * q + 8, :][None]
        for c in range(count):
            finish(c, rows, jnp.sum(sums[c], axis=1))
        return carry

    lax.fori_loop(0, GROUPS, block, 0)


def prepare_kernel(inv_ref, neighbours_ref, partners_ref, u_ref, t_ref, index_ref, nodes_ref, acc_ref,
                   wide, tail, square, line_ref, own, sems, small):
    smalls = [
        pltpu.make_async_copy(u_ref, own, small.at[0]),
        pltpu.make_async_copy(neighbours_ref, square, small.at[1]),
        pltpu.make_async_copy(partners_ref, line_ref, small.at[2]),
    ]
    for copy in smalls:
        copy.start()

    def pieces(g, i, start):
        rows = pl.ds(start, 8)
        return [
            pltpu.make_async_copy(inv_ref.at[:, rows, pl.ds(0, 128)], wide.at[g, 0, i], sems.at[g, i, 0]),
            pltpu.make_async_copy(inv_ref.at[:, rows, pl.ds(128, 128)], wide.at[g, 1, i], sems.at[g, i, 1]),
            pltpu.make_async_copy(inv_ref.at[:, rows, pl.ds(256, 64)], tail.at[g, i], sems.at[g, i, 2]),
        ]

    for g in range(GROUPS):
        f, half = g // 2, g % 2
        for i in range(4):
            for copy in pieces(g, i, f * 64 + i * 16 + half * 8):
                copy.start()
    def turn_group(g, carry):
        for i in range(4):
            for copy in pieces(g, i, 0):
                copy.wait()
        for r in range(8):
            rows = pl.ds(r, LANES, stride=8)
            t_ref[g * 8 + r, 0:128] = wide.at[g, 0].reshape(1024, LANES)[rows, :].T
            t_ref[g * 8 + r, 128:256] = wide.at[g, 1].reshape(1024, LANES)[rows, :].T
            t_ref[g * 8 + r, 256:320] = tail[g, :, :, r, :].reshape(LANES, 64).T
        return carry

    lax.fori_loop(0, GROUPS, turn_group, 0)
    for copy in smalls:
        copy.wait()
    count = lax.axis_size("elem")
    rank = lax.axis_index("elem")
    base = lane() % 32
    turned = jnp.concatenate([square[...]] * 4, axis=1)

    def slots(values, first):
        block = lax.shift_right_logical(values, 5) - rank - first
        block = jnp.where(block < 0, block + count, block)
        block = jnp.where(block < 0, block + count, block)
        block = jnp.where(block >= count, block - count, block)
        return block * ELEMS + (values & 31)

    near = slots(turned, -1)
    for face in range(5):
        index_ref[face] = jnp.broadcast_to(near[face : face + 1], (8, LANES))
    line = jnp.broadcast_to(line_ref[pl.ds(rank // 4, 1), :], (8, LANES))
    line = jnp.take_along_axis(line, base + (rank % 4) * 32, axis=1, mode="promise_in_bounds")
    index_ref[5] = slots(line, count // 4)
    u = flipped(jnp.concatenate([own[...]] * 4, axis=0))
    nodes_ref[...] = u
    acc_ref[...] = volume(u)


def first_kernel(t_ref, index_ref, nodes_ref, acc_ref, moved,
                 x_ref, nx_ref, ny_ref, nz_ref, v_ref):
    before, after, ahead, beyond = pulled(moved)
    near = flipped(jnp.concatenate([before, before, after, after], axis=0))
    near = jnp.where(lane() // 32 == 1, nodes_ref[...], near)
    far = flipped(jnp.concatenate([ahead, beyond] * 2, axis=0))
    nx, ny, nz = aligned(near, far, index_ref[...])
    nx_ref[...], ny_ref[...], nz_ref[...] = nx, ny, nz
    total = acc_ref[...] + face_terms(nodes_ref[...], nx, ny, nz)
    v_ref[0] = (-2.0 * total).reshape(UNK, LANES)

    def finish(c, rows, value):
        x_ref[rows, :] = value

    multiply(t_ref, v_ref, x_ref, 1, finish)


def second_kernel(t_ref, index_ref, own_ref, moved,
                  y_ref, nx_ref, ny_ref, nz_ref, v_ref):
    near, far = near_far(own_ref[...], *pulled(moved))
    nx, ny, nz = aligned(near, far, index_ref[...])
    nx_ref[...], ny_ref[...], nz_ref[...] = nx, ny, nz
    v_ref[0] = lifted(nx, ny, nz).reshape(UNK, LANES)

    def finish(c, rows, value):
        y_ref[rows, :] = value

    multiply(t_ref, v_ref, y_ref, 1, finish)


def section_value(table, which):
    first = lax.axis_index("section") == 0
    return jnp.where(first, table[which], table[2 + which]).astype(jnp.float32)


def middle_kernel(u_ref, x_ref, y_ref, ux_ref, uy_ref, uz_ref, xx_ref, xy_ref, xz_ref,
                  states_ref, acc_ref, nx_ref, ny_ref, nz_ref, part_ref, base_ref):
    u = u_ref[...]
    x, y = spread(x_ref[...]), spread(y_ref[...])
    a = by_group(STEP_X)
    states = u + a * x + by_group(STEP_Y) * y
    states_ref[...] = states
    acc_ref[...] = volume(states)
    nx_ref[...] = ux_ref[...] + a * xx_ref[...]
    ny_ref[...] = uy_ref[...] + a * xy_ref[...]
    nz_ref[...] = uz_ref[...] + a * xz_ref[...]
    compact = squeezed(u)
    for c in range(2):
        part_ref[c] = -section_value(STEP_X, c) * x - section_value(STEP_Y, c) * y
        base_ref[c] = compact + section_value(STEP_X, c) * x_ref[...] + section_value(STEP_Y, c) * y_ref[...]


def third_kernel(t_ref, index_ref, states_ref, acc_ref, nx_ref, ny_ref, nz_ref, part_ref, base_ref,
                 own_ref, moved, first_ref, sum_ref, v_ref):
    near, far = near_far(own_ref[...], *pulled(moved))
    yx, yy, yz = aligned(near, far, index_ref[...])
    b = by_group(STEP_Y)
    total = acc_ref[...] + face_terms(
        states_ref[...], nx_ref[...] + b * yx, ny_ref[...] + b * yy, nz_ref[...] + b * yz
    )
    turned = [total] + [roll_lanes(total, 32 * r) for r in (1, 2, 3)]
    for c in range(2):
        v = part_ref[c]
        for r in range(4):
            factor = by_group(
                [
                    section_value([-2.0 * time_step * BUTCHER[s][(g - r) % 4] for s in range(4)], c)
                    for g in range(4)
                ]
            )
            v = v + factor * turned[r]
        v_ref[c] = v.reshape(UNK, LANES)

    def finish(c, rows, value):
        first_ref[c, rows, :] = value
        sum_ref[c, rows, :] = base_ref[c, rows, :] + value

    multiply(t_ref, v_ref, first_ref, 2, finish)


def fourth_kernel(t_ref, index_ref, base_ref, own_ref, moved, out_ref, v_ref, done_ref):
    for c in range(2):
        near, far = near_far(own_ref[c], *pulled(moved, c))
        v_ref[c] = lifted(*aligned(near, far, index_ref[...])).reshape(UNK, LANES)

    def finish(c, rows, value):
        done_ref[c, rows, :] = base_ref[c, rows, :] + section_value(COUPLING, c) * value

    multiply(t_ref, v_ref, done_ref, 2, finish)
    both = nodes_of([group_of([done_ref[0], done_ref[1]], [i] * 2) for i in range(4)]).reshape(UNK, LANES)
    turned = [
        both[0:128].T,
        both[128:256].T,
        jnp.concatenate([both[256:320], both[256:320]], axis=0).T[:, :64],
    ]
    for c in range(2):
        rows = slice(c * ELEMS, (c + 1) * ELEMS)
        out_ref[c, :, 0:128] = turned[0][rows]
        out_ref[c, :, 128:256] = turned[1][rows]
        out_ref[c, :, 256:320] = turned[2][rows]


VMEM = pltpu.VMEM
F32 = jnp.float32
NODES = (FIELDS, 4, 2, 8, LANES)
NX = (FIELDS, 2, 2, 8, LANES)
COMPACT = (ROWS, LANES)


def call(kernel, inputs, outputs, scratch=(), anywhere=(), flops=10**7, room=8):
    in_specs = [pl.BlockSpec(memory_space=pltpu.HBM if i in anywhere else VMEM) for i in range(len(inputs))]
    return pl.pallas_call(
        kernel,
        out_shape=outputs,
        in_specs=in_specs,
        out_specs=[pl.BlockSpec(memory_space=VMEM)] * len(outputs),
        scratch_shapes=list(scratch),
        compiler_params=pltpu.CompilerParams(vmem_limit_bytes=room * 2**20),
        cost_estimate=pl.CostEstimate(flops=flops, bytes_accessed=10**6, transcendentals=0),
    )(*inputs)


def vm(shape, dtype=F32):
    return pltpu.VMEM(shape, dtype)


def routes(count):
    far = count // 4
    return {
        "before": [(i - 1) % count for i in range(count)],
        "after": [(i + 1) % count for i in range(count)],
        "inner": [i ^ 1 for i in range(count)],
        "outer": [(i - 1 + 2 * (i % 2)) % count for i in range(count)],
        "ahead": [(i + far) % count for i in range(count)],
        "beyond": [(i + far + 1) % count for i in range(count)],
    }


def pulled(moved, at=Ellipsis):
    got = {name: ref[at] for name, ref in moved.items()}
    if "inner" in got:
        odd = lax.axis_index("elem") % 2 == 1
        got["before"] = jnp.where(odd, got["inner"], got["outer"])
        got["after"] = jnp.where(odd, got["outer"], got["inner"])
    return got["before"], got["after"], got["ahead"], got["beyond"]


def exchanged(block, order):
    table = routes(lax.axis_size("elem"))
    return {name: lax.ppermute(block, "elem", [(s, i) for i, s in enumerate(table[name])]) for name in order}


def with_moved(kernel, inputs, moved, outputs, scratch):
    count = len(inputs)
    names = list(moved)

    def whole(*refs):
        kernel(*refs[:count], dict(zip(names, refs[count:])), *refs[count + len(names) :])

    return call(whole, [*inputs, *moved.values()], outputs, scratch)


def keep(x):
    return pltpu.with_memory_space_constraint(x, VMEM)


def on_device(u_start, inverses, neighbours, partners):
    partners = partners.reshape(-1, LANES)
    u_moved = exchanged(u_start, ORDERS[0])
    t, index, nodes, acc = call(
        prepare_kernel,
        [pltpu.with_memory_space_constraint(k, pltpu.HBM) for k in (inverses, neighbours.T, partners, u_start)],
        [vm((ROWS, UNK, LANES)), vm((6, 8, LANES), jnp.int32), vm(NODES), vm(NODES)],
        [
            pltpu.VMEM((GROUPS, 2, 4, ELEMS, 8, LANES), F32),
            pltpu.VMEM((GROUPS, 4, ELEMS, 8, 64), F32),
            pltpu.VMEM((5, ELEMS), jnp.int32),
            pltpu.VMEM((partners.shape[0], LANES), jnp.int32),
            pltpu.VMEM((ELEMS, UNK), F32),
            pltpu.SemaphoreType.DMA((GROUPS, 4, 3)),
            pltpu.SemaphoreType.DMA((3,)),
        ],
        anywhere=(0, 1, 2, 3),
        flops=10**9,
        room=24,
    )
    t, index, nodes = keep(t), keep(index), keep(nodes)
    single = [pltpu.VMEM((1, UNK, LANES), F32)]
    faces = [vm(COMPACT), vm(NX), vm(NODES), vm(NODES)]
    x, ux, uy, uz = with_moved(first_kernel, [t, index, nodes, keep(acc)], u_moved, faces, single)
    y, xx, xy, xz = with_moved(second_kernel, [t, index, x], exchanged(x, ORDERS[1]), faces, single)
    y_moved = exchanged(y, ORDERS[2])
    states, acc, nx, ny, nz, part, base = call(
        middle_kernel,
        [nodes, keep(x), keep(y), *[keep(k) for k in (ux, uy, uz, xx, xy, xz)]],
        [vm(NODES), vm(NODES), vm(NX), vm(NODES), vm(NODES), vm((2,) + NODES), vm((2,) + COMPACT)],
    )
    first, base = with_moved(
        third_kernel,
        [t, index, *[keep(k) for k in (states, acc, nx, ny, nz, part, base)], y],
        y_moved,
        [vm((2,) + COMPACT), vm((2,) + COMPACT)],
        [pltpu.VMEM((2, UNK, LANES), F32)],
    )
    [out] = with_moved(
        fourth_kernel,
        [t, index, keep(base), first],
        exchanged(first, ORDERS[3]),
        [jax.ShapeDtypeStruct((2, ELEMS, UNK), F32)],
        [pltpu.VMEM((2, UNK, LANES), F32), pltpu.VMEM((2,) + COMPACT, F32)],
    )
    return out


def solution(mesh):
    placed = (P("elem", None), P("elem", None, None), P("elem", None), P())
    return jax.shard_map(
        on_device, mesh=mesh, in_specs=placed, out_specs=P("section", "elem", None), check_vma=False
    )
```

```python
import functools
import math

import jax
import jax.numpy as jnp
from jax import lax
from jax.experimental import pallas as pl
from jax.experimental.pallas import tpu as pltpu
from jax.sharding import PartitionSpec as P

ELEMS = 32
FIELDS = 5
UNK = 320
ROWS = 80
LANES = 128
GROUPS = 10
SECTIONS = 4

time_step = 0.03
dissipation = 2.0
enthalpy_factor = 3.5
radau_nodes = [0.08858795951270394, 0.4094668644407347, 0.787659461760847, 1.0]


def lobatto():
    inner = 1.0 / math.sqrt(5.0)
    nodes = [-1.0, -inner, inner, 1.0]
    products = []
    for row in range(4):
        value = 1.0
        for other in range(4):
            if other != row:
                value = value * (nodes[row] - nodes[other])
        products.append(value)
    return [
        [
            0.0 if row == column
            else 2.0 * (products[row] / products[column]) / (nodes[row] - nodes[column])
            for column in range(4)
        ]
        for row in range(4)
    ]


def radau_table():
    columns = []
    for column in range(SECTIONS):
        coeffs = [1.0]
        scale = 1.0
        for other in range(SECTIONS):
            if other != column:
                shifted = [0.0] + coeffs
                for position in range(len(coeffs)):
                    shifted[position] = shifted[position] - radau_nodes[other] * coeffs[position]
                coeffs = shifted
                scale = scale * (radau_nodes[column] - radau_nodes[other])
        columns.append([0.0] + [c / (k + 1.0) / scale for k, c in enumerate(coeffs)])
    butcher = []
    for row in range(SECTIONS):
        entries = []
        for column in range(SECTIONS):
            value = 0.0
            for coefficient in reversed(columns[column]):
                value = value * radau_nodes[row] + coefficient
            entries.append(value)
        butcher.append(entries)
    return butcher


DERIV = lobatto()
WEIGHT = 6.0
BUTCHER = radau_table()
ROW_SUM = [sum(row) for row in BUTCHER]
COUPLING = [time_step * BUTCHER[i][i] * dissipation * WEIGHT for i in range(SECTIONS)]
STEP_X = [time_step * ROW_SUM[i] for i in range(SECTIONS)]
STEP_Y = [time_step * ROW_SUM[i] * COUPLING[i] for i in range(SECTIONS)]

ORDERS = [('before', 'ahead', 'beyond', 'after'), ('beyond', 'ahead', 'after', 'before'), ('after', 'before', 'beyond', 'ahead'), ('ahead', 'beyond', 'after', 'before')]


def sublane():
    return lax.broadcasted_iota(jnp.int32, (8, LANES), 0)


def lane():
    return lax.broadcasted_iota(jnp.int32, (8, LANES), 1)


def by_row(values):
    s = sublane()
    out = jnp.full((8, LANES), values[7], jnp.float32)
    for row in range(6, -1, -1):
        out = jnp.where(s == row, values[row], out)
    return out


def by_group(values):
    group = lane() // 32
    out = jnp.full((8, LANES), values[3], jnp.float32)
    for g in range(2, -1, -1):
        out = jnp.where(group == g, values[g], out)
    return out


def roll_rows(x, shift):
    shape = x.shape
    y = x.reshape(-1, 8, LANES)
    return pltpu.roll(y, shift % 8, axis=1).reshape(shape)


def roll_lanes(x, shift):
    if shift % LANES == 0:
        return x
    shape = x.shape
    y = x.reshape(-1, LANES)
    return pltpu.roll(y, shift % LANES, axis=1).reshape(shape)


def pick_lanes(x, index):
    shape = x.shape
    y = x.reshape(-1, LANES)
    wide = jnp.broadcast_to(index[None], (y.shape[0] // 8, 8, LANES)).reshape(y.shape)
    return jnp.take_along_axis(y, wide, axis=1, mode="promise_in_bounds").reshape(shape)


def prepared(u):
    half = [0.5 * u[f] for f in range(FIELDS)]
    square = half[1] * half[1] + half[2] * half[2] + half[3] * half[3]
    return half + [enthalpy_factor * half[4], square]


def take(state, index):
    return [x[index] for x in state]


def pair_flux(a, b, direction):
    density, v0, v1, v2, pressure, energy, square = [x + y for x, y in zip(a, b)]
    velocity = [v0, v1, v2]
    normal = velocity[direction]
    mass = density * normal
    out = [mass]
    for comp in range(3):
        momentum = mass * velocity[comp]
        out.append(momentum + pressure if comp == direction else momentum)
    out.append(normal * (energy + density * square))
    return out


def volume(u):
    n = prepared(u)
    d = DERIV
    rows = [[None] * 4 for _ in range(FIELDS)]

    def add(f, i, value):
        rows[f][i] = value if rows[f][i] is None else rows[f][i] + value

    for i in range(4):
        for other in range(i + 1, 4):
            flux = pair_flux(take(n, i), take(n, other), 0)
            for f in range(FIELDS):
                add(f, i, d[i][other] * flux[f])
                add(f, other, d[other][i] * flux[f])
    low = [(s // 4) for s in range(8)]
    c_same_low = by_row([d[j][1 - j] for j in low])
    c_same_high = by_row([d[2 + j][3 - j] for j in low])
    c_up = by_row([d[j][2 + j] for j in low])
    c_down = by_row([d[2 + j][j] for j in low])
    c_up_turn = by_row([d[j][3 - j] for j in low])
    c_down_turn = by_row([d[2 + j][1 - j] for j in low])
    c_next = [by_row([d[s % 4][(s % 4 + r) % 4] for s in range(8)]) for r in (1, 2, 3)]
    within = sublane() % 4

    def spin(x, r):
        return jnp.where(within + r < 4, roll_rows(x, 8 - r), roll_rows(x, 4 - r))

    for i in range(4):
        a = [x[i, 0] for x in n]
        b = [x[i, 1] for x in n]
        ra = [roll_rows(x, 4) for x in a]
        rb = [roll_rows(x, 4) for x in b]
        f1 = pair_flux(a, ra, 1)
        f2 = pair_flux(b, rb, 1)
        f3 = pair_flux(a, b, 1)
        f4 = pair_flux(a, rb, 1)
        f5 = pair_flux(b, ra, 1)
        n_i = [x[i] for x in n]
        z1 = pair_flux(n_i, [spin(x, 1) for x in n_i], 2)
        z2 = pair_flux(n_i, [spin(x, 2) for x in n_i], 2)
        for f in range(FIELDS):
            upper = c_same_low * f1[f] + c_up * f3[f] + c_up_turn * f4[f]
            lower = c_same_high * f2[f] + c_down * f3[f] + c_down_turn * f5[f]
            add(f, i, jnp.stack([upper, lower]))
            add(f, i, c_next[0] * z1[f] + c_next[1] * z2[f] + c_next[2] * spin(z1[f], 3))
    return jnp.stack([jnp.stack(rows[f]) for f in range(FIELDS)])


def face_terms(u, nx, ny, nz):
    n = prepared(u)
    px, py, pz = prepared(nx), prepared(ny), prepared(nz)
    half = 0.5 * dissipation
    s = sublane()
    low_x = pair_flux(take(n, 0), [x[0] for x in px], 0)
    high_x = pair_flux(take(n, 3), [x[1] for x in px], 0)
    y0 = pair_flux([x[:, 0] for x in n], [x[:, 0] for x in py], 1)
    y1 = pair_flux([x[:, 1] for x in n], [x[:, 1] for x in py], 1)
    z = pair_flux(n, pz, 2)
    k = s % 4
    sign_z = jnp.where(k == 0, -WEIGHT, WEIGHT)
    on_z = (k == 0) | (k == 3)
    out = []
    for f in range(FIELDS):
        part_z = jnp.where(on_z, sign_z * z[f] - (WEIGHT * half) * (nz[f] - u[f]), 0.0)
        part_y0 = jnp.where(s < 4, -WEIGHT * y0[f] - (WEIGHT * half) * (ny[f][:, 0] - u[f][:, 0]), 0.0)
        part_y1 = jnp.where(s < 4, 0.0, WEIGHT * y1[f] - (WEIGHT * half) * (ny[f][:, 1] - u[f][:, 1]))
        total = part_z + jnp.stack([part_y0, part_y1], axis=1)
        x0 = -WEIGHT * low_x[f] - (WEIGHT * half) * (nx[f][0] - u[f][0])
        x3 = WEIGHT * high_x[f] - (WEIGHT * half) * (nx[f][1] - u[f][3])
        out.append(jnp.stack([total[0] + x0, total[1], total[2], total[3] + x3]))
    return jnp.stack(out)


def lifted(nx, ny, nz):
    s = sublane()
    k = s % 4
    y = jnp.stack([jnp.where(s < 4, ny[:, :, 0], 0.0), jnp.where(s < 4, 0.0, ny[:, :, 1])], axis=2)
    total = y + jnp.where((k == 0) | (k == 3), nz, 0.0)
    return jnp.stack([total[:, 0] + nx[:, 0], total[:, 1], total[:, 2], total[:, 3] + nx[:, 1]], axis=1)


def aligned(near, far, index):
    nx = jnp.stack([pick_lanes(near[:, 3], index[0]), pick_lanes(near[:, 0], index[1])], axis=1)
    ny = jnp.stack(
        [
            roll_rows(pick_lanes(near[:, :, 1], index[2]), 4),
            roll_rows(pick_lanes(near[:, :, 0], index[3]), 4),
        ],
        axis=2,
    )
    lower = roll_rows(pick_lanes(near, index[4]), 5)
    upper = roll_rows(pick_lanes(far, index[5]), 3)
    nz = jnp.where(sublane() % 4 == 0, lower, upper)
    return nx, ny, nz


def nodes_of(parts):
    return jnp.stack([p.reshape(FIELDS, 2, 8, LANES) for p in parts], axis=1)


def group_of(x, groups):
    at = lane()[:1] // 32
    parts = [roll_lanes(y, 32 * (g - group)) for g, (y, group) in enumerate(zip(x, groups))]
    out = parts[-1]
    for g in range(len(parts) - 2, -1, -1):
        out = jnp.where(at == g, parts[g], out)
    return out


def near_far(own, before, after, ahead, beyond):
    near = nodes_of([group_of([before, own, after], [i] * 3) for i in range(4)])
    far = nodes_of([group_of([ahead, beyond], [i] * 2) for i in range(4)])
    return near, far


def spread(compact):
    base = lane() % 32
    return nodes_of([pick_lanes(compact, base + 32 * i) for i in range(4)])


def squeezed(nodes):
    at = lane() // 32
    parts = [nodes[:, i].reshape(ROWS // 8, 8, LANES) for i in range(4)]
    out = parts[3]
    for i in range(2, -1, -1):
        out = jnp.where(at == i, parts[i], out)
    return out.reshape(ROWS, LANES)


def flipped(x):
    pieces = [
        x[:, 0:128].T,
        x[:, 128:256].T,
        jnp.concatenate([x[:, 256:320], jnp.zeros((LANES, 64), jnp.float32)], axis=1).T[:64],
    ]
    return jnp.concatenate(pieces, axis=0).reshape(FIELDS, 4, 2, 8, LANES)


def multiply(t_ref, v_ref, out_ref, count, finish):
    def block(g, carry):
        rows = pl.ds(pl.multiple_of(g * 8, 8), 8)
        sums = [jnp.zeros((8, 8, LANES), jnp.float32) for _ in range(count)]
        for q in range(UNK // 8):
            piece = t_ref[rows, 8 * q : 8 * q + 8, :]
            for c in range(count):
                sums[c] = sums[c] + piece * v_ref[c, 8 * q : 8 * q + 8, :][None]
        for c in range(count):
            finish(c, rows, jnp.sum(sums[c], axis=1))
        return carry

    lax.fori_loop(0, GROUPS, block, 0)


def prepare_kernel(inv_ref, neighbours_ref, partners_ref, u_ref, t_ref, index_ref, nodes_ref, acc_ref,
                   wide, tail, square, line_ref, own, sems, small):
    smalls = [
        pltpu.make_async_copy(u_ref, own, small.at[0]),
        pltpu.make_async_copy(neighbours_ref, square, small.at[1]),
        pltpu.make_async_copy(partners_ref, line_ref, small.at[2]),
    ]
    for copy in smalls:
        copy.start()

    def pieces(g, i, start):
        rows = pl.ds(start, 8)
        return [
            pltpu.make_async_copy(inv_ref.at[:, rows, pl.ds(0, 128)], wide.at[g, 0, i], sems.at[g, i, 0]),
            pltpu.make_async_copy(inv_ref.at[:, rows, pl.ds(128, 128)], wide.at[g, 1, i], sems.at[g, i, 1]),
            pltpu.make_async_copy(inv_ref.at[:, rows, pl.ds(256, 64)], tail.at[g, i], sems.at[g, i, 2]),
        ]

    for g in range(GROUPS):
        f, half = g // 2, g % 2
        for i in range(4):
            for copy in pieces(g, i, f * 64 + i * 16 + half * 8):
                copy.start()
    def turn_group(g, carry):
        for i in range(4):
            for copy in pieces(g, i, 0):
                copy.wait()
        for r in range(8):
            rows = pl.ds(r, LANES, stride=8)
            t_ref[g * 8 + r, 0:128] = wide.at[g, 0].reshape(1024, LANES)[rows, :].T
            t_ref[g * 8 + r, 128:256] = wide.at[g, 1].reshape(1024, LANES)[rows, :].T
            t_ref[g * 8 + r, 256:320] = tail[g, :, :, r, :].reshape(LANES, 64).T
        return carry

    lax.fori_loop(0, GROUPS, turn_group, 0)
    for copy in smalls:
        copy.wait()
    count = lax.axis_size("elem")
    rank = lax.axis_index("elem")
    base = lane() % 32
    turned = jnp.concatenate([square[...]] * 4, axis=1)

    def slots(values, first):
        block = lax.shift_right_logical(values, 5) - rank - first
        block = jnp.where(block < 0, block + count, block)
        block = jnp.where(block < 0, block + count, block)
        block = jnp.where(block >= count, block - count, block)
        return block * ELEMS + (values & 31)

    near = slots(turned, -1)
    for face in range(5):
        index_ref[face] = jnp.broadcast_to(near[face : face + 1], (8, LANES))
    line = jnp.broadcast_to(line_ref[pl.ds(rank // 4, 1), :], (8, LANES))
    line = jnp.take_along_axis(line, base + (rank % 4) * 32, axis=1, mode="promise_in_bounds")
    index_ref[5] = slots(line, count // 4)
    u = flipped(jnp.concatenate([own[...]] * 4, axis=0))
    nodes_ref[...] = u
    acc_ref[...] = volume(u)


def first_kernel(t_ref, index_ref, nodes_ref, acc_ref, moved,
                 x_ref, nx_ref, ny_ref, nz_ref, v_ref):
    before, after, ahead, beyond = pulled(moved)
    near = flipped(jnp.concatenate([before, before, after, after], axis=0))
    near = jnp.where(lane() // 32 == 1, nodes_ref[...], near)
    far = flipped(jnp.concatenate([ahead, beyond] * 2, axis=0))
    nx, ny, nz = aligned(near, far, index_ref[...])
    nx_ref[...], ny_ref[...], nz_ref[...] = nx, ny, nz
    total = acc_ref[...] + face_terms(nodes_ref[...], nx, ny, nz)
    v_ref[0] = (-2.0 * total).reshape(UNK, LANES)

    def finish(c, rows, value):
        x_ref[rows, :] = value

    multiply(t_ref, v_ref, x_ref, 1, finish)


def second_kernel(t_ref, index_ref, own_ref, moved,
                  y_ref, nx_ref, ny_ref, nz_ref, v_ref):
    near, far = near_far(own_ref[...], *pulled(moved))
    nx, ny, nz = aligned(near, far, index_ref[...])
    nx_ref[...], ny_ref[...], nz_ref[...] = nx, ny, nz
    v_ref[0] = lifted(nx, ny, nz).reshape(UNK, LANES)

    def finish(c, rows, value):
        y_ref[rows, :] = value

    multiply(t_ref, v_ref, y_ref, 1, finish)


def section_value(table, which):
    first = lax.axis_index("section") == 0
    return jnp.where(first, table[which], table[2 + which]).astype(jnp.float32)


def middle_kernel(u_ref, x_ref, y_ref, ux_ref, uy_ref, uz_ref, xx_ref, xy_ref, xz_ref,
                  states_ref, acc_ref, nx_ref, ny_ref, nz_ref, part_ref, base_ref):
    u = u_ref[...]
    x, y = spread(x_ref[...]), spread(y_ref[...])
    a = by_group(STEP_X)
    states = u + a * x + by_group(STEP_Y) * y
    states_ref[...] = states
    acc_ref[...] = volume(states)
    nx_ref[...] = ux_ref[...] + a * xx_ref[...]
    ny_ref[...] = uy_ref[...] + a * xy_ref[...]
    nz_ref[...] = uz_ref[...] + a * xz_ref[...]
    compact = squeezed(u)
    for c in range(2):
        part_ref[c] = -section_value(STEP_X, c) * x - section_value(STEP_Y, c) * y
        base_ref[c] = compact + section_value(STEP_X, c) * x_ref[...] + section_value(STEP_Y, c) * y_ref[...]


def third_kernel(t_ref, index_ref, states_ref, acc_ref, nx_ref, ny_ref, nz_ref, part_ref, base_ref,
                 own_ref, moved, first_ref, sum_ref, v_ref):
    near, far = near_far(own_ref[...], *pulled(moved))
    yx, yy, yz = aligned(near, far, index_ref[...])
    b = by_group(STEP_Y)
    total = acc_ref[...] + face_terms(
        states_ref[...], nx_ref[...] + b * yx, ny_ref[...] + b * yy, nz_ref[...] + b * yz
    )
    turned = [total] + [roll_lanes(total, 32 * r) for r in (1, 2, 3)]
    for c in range(2):
        v = part_ref[c]
        for r in range(4):
            factor = by_group(
                [
                    section_value([-2.0 * time_step * BUTCHER[s][(g - r) % 4] for s in range(4)], c)
                    for g in range(4)
                ]
            )
            v = v + factor * turned[r]
        v_ref[c] = v.reshape(UNK, LANES)

    def finish(c, rows, value):
        first_ref[c, rows, :] = value
        sum_ref[c, rows, :] = base_ref[c, rows, :] + value

    multiply(t_ref, v_ref, first_ref, 2, finish)


def fourth_kernel(t_ref, index_ref, base_ref, own_ref, moved, out_ref, v_ref, done_ref):
    for c in range(2):
        near, far = near_far(own_ref[c], *pulled(moved, c))
        v_ref[c] = lifted(*aligned(near, far, index_ref[...])).reshape(UNK, LANES)

    def finish(c, rows, value):
        done_ref[c, rows, :] = base_ref[c, rows, :] + section_value(COUPLING, c) * value

    multiply(t_ref, v_ref, done_ref, 2, finish)
    both = nodes_of([group_of([done_ref[0], done_ref[1]], [i] * 2) for i in range(4)]).reshape(UNK, LANES)
    turned = [
        both[0:128].T,
        both[128:256].T,
        jnp.concatenate([both[256:320], both[256:320]], axis=0).T[:, :64],
    ]
    for c in range(2):
        rows = slice(c * ELEMS, (c + 1) * ELEMS)
        out_ref[c, :, 0:128] = turned[0][rows]
        out_ref[c, :, 128:256] = turned[1][rows]
        out_ref[c, :, 256:320] = turned[2][rows]


VMEM = pltpu.VMEM
F32 = jnp.float32
NODES = (FIELDS, 4, 2, 8, LANES)
NX = (FIELDS, 2, 2, 8, LANES)
COMPACT = (ROWS, LANES)


def call(kernel, inputs, outputs, scratch=(), anywhere=(), flops=10**7, room=8):
    in_specs = [pl.BlockSpec(memory_space=pltpu.HBM if i in anywhere else VMEM) for i in range(len(inputs))]
    return pl.pallas_call(
        kernel,
        out_shape=outputs,
        in_specs=in_specs,
        out_specs=[pl.BlockSpec(memory_space=VMEM)] * len(outputs),
        scratch_shapes=list(scratch),
        compiler_params=pltpu.CompilerParams(vmem_limit_bytes=room * 2**20),
        cost_estimate=pl.CostEstimate(flops=flops, bytes_accessed=10**6, transcendentals=0),
    )(*inputs)


def vm(shape, dtype=F32):
    return pltpu.VMEM(shape, dtype)


def routes(count):
    far = count // 4
    return {
        "before": [(i - 1) % count for i in range(count)],
        "after": [(i + 1) % count for i in range(count)],
        "inner": [i ^ 1 for i in range(count)],
        "outer": [(i - 1 + 2 * (i % 2)) % count for i in range(count)],
        "ahead": [(i + far) % count for i in range(count)],
        "beyond": [(i + far + 1) % count for i in range(count)],
    }


def pulled(moved, at=Ellipsis):
    got = {name: ref[at] for name, ref in moved.items()}
    if "inner" in got:
        odd = lax.axis_index("elem") % 2 == 1
        got["before"] = jnp.where(odd, got["inner"], got["outer"])
        got["after"] = jnp.where(odd, got["outer"], got["inner"])
    return got["before"], got["after"], got["ahead"], got["beyond"]


def exchanged(block, order):
    table = routes(lax.axis_size("elem"))
    return {name: lax.ppermute(block, "elem", [(s, i) for i, s in enumerate(table[name])]) for name in order}


def with_moved(kernel, inputs, moved, outputs, scratch):
    count = len(inputs)
    names = list(moved)

    def whole(*refs):
        kernel(*refs[:count], dict(zip(names, refs[count:])), *refs[count + len(names) :])

    return call(whole, [*inputs, *moved.values()], outputs, scratch)


def keep(x):
    return pltpu.with_memory_space_constraint(x, VMEM)


def on_device(u_start, inverses, neighbours, partners):
    partners = partners.reshape(-1, LANES)
    u_moved = exchanged(u_start, ORDERS[0])
    t, index, nodes, acc = call(
        prepare_kernel,
        [pltpu.with_memory_space_constraint(k, pltpu.HBM) for k in (inverses, neighbours.T, partners, u_start)],
        [vm((ROWS, UNK, LANES)), vm((6, 8, LANES), jnp.int32), vm(NODES), vm(NODES)],
        [
            pltpu.VMEM((GROUPS, 2, 4, ELEMS, 8, LANES), F32),
            pltpu.VMEM((GROUPS, 4, ELEMS, 8, 64), F32),
            pltpu.VMEM((5, ELEMS), jnp.int32),
            pltpu.VMEM((partners.shape[0], LANES), jnp.int32),
            pltpu.VMEM((ELEMS, UNK), F32),
            pltpu.SemaphoreType.DMA((GROUPS, 4, 3)),
            pltpu.SemaphoreType.DMA((3,)),
        ],
        anywhere=(0, 1, 2, 3),
        flops=10**9,
        room=24,
    )
    t, index, nodes = keep(t), keep(index), keep(nodes)
    single = [pltpu.VMEM((1, UNK, LANES), F32)]
    faces = [vm(COMPACT), vm(NX), vm(NODES), vm(NODES)]
    x, ux, uy, uz = with_moved(first_kernel, [t, index, nodes, keep(acc)], u_moved, faces, single)
    y, xx, xy, xz = with_moved(second_kernel, [t, index, x], exchanged(x, ORDERS[1]), faces, single)
    y_moved = exchanged(y, ORDERS[2])
    states, acc, nx, ny, nz, part, base = call(
        middle_kernel,
        [nodes, keep(x), keep(y), *[keep(k) for k in (ux, uy, uz, xx, xy, xz)]],
        [vm(NODES), vm(NODES), vm(NX), vm(NODES), vm(NODES), vm((2,) + NODES), vm((2,) + COMPACT)],
    )
    first, base = with_moved(
        third_kernel,
        [t, index, *[keep(k) for k in (states, acc, nx, ny, nz, part, base)], y],
        y_moved,
        [vm((2,) + COMPACT), vm((2,) + COMPACT)],
        [pltpu.VMEM((2, UNK, LANES), F32)],
    )
    [out] = with_moved(
        fourth_kernel,
        [t, index, keep(base), first],
        exchanged(first, ORDERS[3]),
        [jax.ShapeDtypeStruct((2, ELEMS, UNK), F32)],
        [pltpu.VMEM((2, UNK, LANES), F32), pltpu.VMEM((2,) + COMPACT, F32)],
    )
    return out


def solution(mesh):
    placed = (P("elem", None), P("elem", None, None), P("elem", None), P())
    return jax.shard_map(
        on_device, mesh=mesh, in_specs=placed, out_specs=P("section", "elem", None), check_vma=False
    )
```
